256 devices in a mesh: role: 2 (over core), seq: 32 (over z, y), tp: 4 (over x).
Axes of the slice: x: 4, y: 4, z: 8, core: 2. Of those that a mesh axis runs over, the one named last changes fastest.
Arguments:
- span_hidden: bfloat16 [2, 8192, 5120], P('role', 'seq'), may hold values from -6 to 6
- attn_gain: float32 [5120], replicated, may hold values from 0.25 to 1.75
- kv_weight: bfloat16 [5120, 2, 1024], P(None, None, 'tp'), may hold values from -0.078125 to 0.078125
- q_gain: float32 [128], replicated, may hold values from 0.5 to 16
- key_norm_gain: float32 [128], replicated, may hold values from 0.5 to 16
- q_weight: bfloat16 [5120, 8192], P('seq', 'tp'), may hold values from -0.078125 to 0.078125
- o_weight: bfloat16 [8192, 5120], P('tp', 'seq'), may hold values from -0.0625 to 0.0625
- decode_hidden: bfloat16 [4, 128, 5120], P(None, 'seq'), may hold values from -6 to 6
- cache: bfloat16 [128, 128, 2, 1024], P('seq', None, None, 'tp'), may hold values from -6 to 6
- cache_len: int32 [128], P('seq'), may hold values from 1 to 128
- block_owner: int32 [32, 32], replicated, may hold values from 0 to 31, as said below
- block_slot: int32 [32, 32], replicated, may hold values from 0 to 31, as said below
Outputs:
- kv_sections: bfloat16 [2, 8192, 2, 1024], P('role', 'seq', None, 'tp')
- decode_sections: bfloat16 [2, 4, 128, 5120], P('role', None, 'seq')
The draws below stay inside these ranges and needn't reach their ends.
Inputs may be any that keep to these rules, and one draw needn't show every extreme that they name: `block_owner`: entry (s, j) names the owner of block j of shard s; every owner receives exactly 32 blocks, no shard sends more than 2 to one owner, and some shard sends exactly 2 to one owner. `block_slot`: the blocks that one owner receives have the slots 0 to 31, each once.
All inputs are finite; a program needn't handle non-finite values.
Results may differ from the reference program's by a relative error of at most 0.014.
Values may be sent and summed in bfloat16 or wider, within the bound.
No kernel may reach another device: no remote copies, remote signals or barrier semaphores. Data moves between devices by JAX's collectives and lax.ppermute only.
A program may use at most 64 MiB of HBM per device.

```python
import math
import jax
import jax.numpy as jnp
from jax import lax

D = 5120
QUERY_HEADS = 64
KEY_VALUE_HEADS = 8
HEAD_SIZE = 128
QW = 8192
KEY_HEADS_WIDTH = 1024
BLK = 8
PB = 32
CAP = 2
SPAN_TOKENS = 8192
DECODE_REQUESTS = 128
CONTEXT_LENGTH = 128
STEPS = 4
N_SEQ = 32


def route_tables(key):
    subkeys = jax.random.split(key, 5)
    source_shift = jax.random.permutation(subkeys[0], N_SEQ)
    owner_names = jax.random.permutation(subkeys[1], N_SEQ)
    first_offset = jax.random.randint(subkeys[2], (), 0, N_SEQ)
    block_number = jnp.arange(PB)
    offsets = jnp.where(block_number < CAP, 0, 1 + (block_number - CAP) % (N_SEQ - 1))
    offsets = (offsets + first_offset) % N_SEQ
    block_order = jax.vmap(lambda one_key: jax.random.permutation(one_key, PB))(jax.random.split(subkeys[3], N_SEQ))
    owner_map = owner_names[(source_shift[:, None] + offsets[block_order]) % N_SEQ]
    slot_order = jax.vmap(lambda one_key: jax.random.permutation(one_key, PB))(jax.random.split(subkeys[4], N_SEQ))
    slot_map = slot_order[owner_map, block_order]
    return (owner_map.astype(jnp.int32), slot_map.astype(jnp.int32))


def draw_block_owner(key, part):
    owner_map, slot_map = route_tables(key)
    return owner_map


def draw_block_slot(key, part):
    owner_map, slot_map = route_tables(key)
    return slot_map


def draw_q_gain(key, part):
    key = jax.random.fold_in(key, 21)
    base = jax.random.uniform(key, (HEAD_SIZE,), jnp.float32, 0.5, 1.5)
    return base


def draw_key_norm_gain(key, part):
    key = jax.random.fold_in(key, 22)
    base = jax.random.uniform(key, (HEAD_SIZE,), jnp.float32, 0.5, 1.5)
    return base


def touch_ends(entries, stream_key, least, largest):
    index_at = [jax.random.randint(jax.random.fold_in(stream_key, axis), (), 0, length) for axis, length in enumerate(entries.shape)]
    widest = entries.shape.index(max(entries.shape))
    beside = index_at[:widest] + [(index_at[widest] + 1) % entries.shape[widest]] + index_at[widest + 1:]
    return entries.at[tuple(index_at)].set(least).at[tuple(beside)].set(largest)


def levels(key, extent, cuts, low, high):
    def one(dim, parts):
        draws = jax.random.uniform(jax.random.fold_in(jax.random.fold_in(key, 6), dim), (parts,), jnp.float32, low / len(cuts), high / len(cuts))
        return jnp.repeat(jnp.exp(draws), extent[dim] // parts).reshape((-1,) + (1,) * (len(extent) - dim - 1))

    loudness = one(*cuts[0])
    for cut in cuts[1:]:
        loudness = loudness * one(*cut)
    return loudness


def gaussian(key, extent, scale, most, cuts=(), held_as=jnp.bfloat16):
    drawn = jax.random.normal(key, extent, jnp.float32) * scale
    if len(cuts) > 0:
        drawn = levels(key, extent, cuts, -0.22, 0.18) * drawn
    return jnp.clip(drawn, min=-most, max=most).astype(held_as)


def setup_inputs(seed: int = 0) -> dict:
    key_list = jax.random.split(jax.random.key(seed), 13)
    return {
        "span_hidden": gaussian(key_list[0], (2, SPAN_TOKENS, D), 1.0, 6.0, ((0, 2), (1, 32))),
        "attn_gain": jnp.clip(1.0 + 0.15 * jax.random.normal(key_list[1], (D,), jnp.float32), 0.25, 1.75),
        "kv_weight": gaussian(key_list[2], (D, 2, KEY_HEADS_WIDTH), D ** -0.5, 0.078125, ((2, 4),)),
        "q_gain": draw_q_gain(jax.random.fold_in(key_list[12], 71), 0),
        "key_norm_gain": draw_key_norm_gain(jax.random.fold_in(key_list[12], 71), 0),
        "q_weight": gaussian(key_list[5], (D, QW), D ** -0.5, 0.078125, ((0, 32), (1, 4))),
        "o_weight": gaussian(key_list[6], (QW, D), QW ** -0.5, 0.0625, ((0, 4), (1, 32))),
        "decode_hidden": gaussian(key_list[7], (STEPS, DECODE_REQUESTS, D), 1.0, 6.0, ((1, 32),)),
        "cache": gaussian(key_list[8], (DECODE_REQUESTS, CONTEXT_LENGTH, 2, KEY_HEADS_WIDTH), 1.0, 6.0, ((0, 32), (3, 4))),
        "cache_len": touch_ends(jax.random.randint(key_list[9], (DECODE_REQUESTS,), 1, CONTEXT_LENGTH + 1), jax.random.fold_in(key_list[9], 1), 1, CONTEXT_LENGTH).astype(jnp.int32),
        "block_owner": draw_block_owner(jax.random.fold_in(key_list[12], 71), 0),
        "block_slot": draw_block_slot(jax.random.fold_in(key_list[12], 71), 0),
    }


EPSILON = 1e-06
THETA_BASE = 1000000.0

def row_scaling(values, weights):
    return values * lax.rsqrt(lax.optimization_barrier(jnp.mean(values * values, axis=-1, keepdims=True)) + EPSILON) * weights

def apply_rotary(values, token_position):
    half_dim = values.shape[-1] // 2
    frequency = jnp.exp(jnp.arange(half_dim, dtype=jnp.float32) * (-2.0 * math.log(THETA_BASE) / values.shape[-1]))
    angles = token_position.astype(jnp.float32)[..., None, None] * frequency
    cosine = jnp.cos(angles)
    sine = jnp.sin(angles)
    first_half = values[..., :half_dim]
    second_half = values[..., half_dim:]
    return jnp.concatenate([first_half * cosine - second_half * sine, second_half * cosine + first_half * sine], axis=-1)

def reference(span_hidden, attn_gain, kv_weight, q_gain, key_norm_gain, q_weight, o_weight, decode_hidden, cache, cache_len, block_owner, block_slot):
    span_normed = row_scaling(span_hidden[0].astype(jnp.float32), attn_gain).astype(jnp.bfloat16)
    span_projected = jnp.einsum('td,dcw->tcw', span_normed.astype(jnp.float32), kv_weight.astype(jnp.float32))
    token_positions = jnp.arange(SPAN_TOKENS, dtype=jnp.int32)
    span_key_rows = apply_rotary(row_scaling(span_projected[:, 0].reshape(SPAN_TOKENS, KEY_VALUE_HEADS, HEAD_SIZE), key_norm_gain), token_positions).reshape(SPAN_TOKENS, KEY_HEADS_WIDTH)
    span_kv = jnp.stack([span_key_rows, span_projected[:, 1]], axis=1).astype(jnp.bfloat16)
    blocks = span_kv.reshape(N_SEQ * PB, BLK, 2, KEY_HEADS_WIDTH)
    target = (block_owner * PB + block_slot).reshape(-1).astype(jnp.int32)
    pool = jnp.zeros_like(blocks).at[target].set(blocks).reshape(SPAN_TOKENS, 2, KEY_HEADS_WIDTH)
    kv_sections = jnp.stack([span_kv, pool])
    query_group_width = QUERY_HEADS // KEY_VALUE_HEADS
    scale_factor = HEAD_SIZE ** (-0.5)
    cached_key_rows = cache[:, :, 0].astype(jnp.float32).reshape(DECODE_REQUESTS, CONTEXT_LENGTH, KEY_VALUE_HEADS, HEAD_SIZE)
    cached_value_rows = cache[:, :, 1].astype(jnp.float32).reshape(DECODE_REQUESTS, CONTEXT_LENGTH, KEY_VALUE_HEADS, HEAD_SIZE)
    visible = jnp.arange(CONTEXT_LENGTH, dtype=jnp.int32)[None, :] < cache_len[:, None]
    gathered_keys = []
    gathered_values = []
    results = []
    for step_index in range(STEPS):
        hidden_rows = decode_hidden[step_index]
        normed = row_scaling(hidden_rows.astype(jnp.float32), attn_gain).astype(jnp.bfloat16)
        token_position = cache_len + step_index
        query_raw = jnp.dot(normed, q_weight, preferred_element_type=jnp.float32).reshape(DECODE_REQUESTS, QUERY_HEADS, HEAD_SIZE)
        query_rows = apply_rotary(row_scaling(query_raw, q_gain), token_position).astype(jnp.bfloat16)
        newest_token = jnp.einsum('rd,dcw->rcw', normed.astype(jnp.float32), kv_weight.astype(jnp.float32))
        gathered_keys.append(apply_rotary(row_scaling(newest_token[:, 0].reshape(DECODE_REQUESTS, KEY_VALUE_HEADS, HEAD_SIZE), key_norm_gain), token_position).astype(jnp.bfloat16))
        gathered_values.append(newest_token[:, 1].reshape(DECODE_REQUESTS, KEY_VALUE_HEADS, HEAD_SIZE).astype(jnp.bfloat16))
        new_keys = jnp.stack(gathered_keys, axis=1).astype(jnp.float32)
        new_values = jnp.stack(gathered_values, axis=1).astype(jnp.float32)
        grouped_queries = query_rows.astype(jnp.float32).reshape(DECODE_REQUESTS, KEY_VALUE_HEADS, query_group_width, HEAD_SIZE)
        old_scores = jnp.einsum('rgqd,rcgd->rgqc', grouped_queries, cached_key_rows) * scale_factor
        old_scores = jnp.where(visible[:, None, None, :], old_scores, -jnp.inf)
        new_scores = jnp.einsum('rgqd,rngd->rgqn', grouped_queries, new_keys) * scale_factor
        top = jnp.maximum(lax.optimization_barrier(jnp.max(old_scores, axis=-1, keepdims=True)), lax.optimization_barrier(jnp.max(new_scores, axis=-1, keepdims=True)))
        old_exp = jnp.exp(old_scores - top)
        new_exp = jnp.exp(new_scores - top)
        total = lax.optimization_barrier(jnp.sum(old_exp, axis=-1, keepdims=True)) + lax.optimization_barrier(jnp.sum(new_exp, axis=-1, keepdims=True))
        old_weights = (old_exp / total).astype(jnp.bfloat16).astype(jnp.float32)
        new_weights = (new_exp / total).astype(jnp.bfloat16).astype(jnp.float32)
        mixed = jnp.einsum('rgqc,rcgd->rgqd', old_weights, cached_value_rows) + jnp.einsum('rgqn,rngd->rgqd', new_weights, new_values)
        attended = mixed.reshape(DECODE_REQUESTS, QW).astype(jnp.bfloat16)
        delta = jnp.dot(attended, o_weight, preferred_element_type=jnp.float32)
        results.append((hidden_rows.astype(jnp.float32) + delta).astype(jnp.bfloat16))
    decoded = jnp.stack(results)
    decode_sections = jnp.stack([jnp.zeros_like(decoded), decoded])
    return (kv_sections, decode_sections)
```

```python
import math

import jax
import jax.numpy as jnp
from jax import lax
from jax.sharding import Mesh, PartitionSpec as P

QUERY_HEADS = 64
KEY_VALUE_HEADS = 8
HEAD_SIZE = 128
EPSILON = 1e-06
THETA_BASE = 1000000.0

Z, Y = 8, 4
SEQ = ("z", "y")
BLOCK_TOKENS = 8
CAPACITY = 2
F32, BF16 = jnp.float32, jnp.bfloat16


def row_scaling(values, weights):
    return values * lax.rsqrt(jnp.mean(values * values, axis=-1, keepdims=True) + EPSILON) * weights


def rotary_tables(token_position):
    half_dim = HEAD_SIZE // 2
    frequency = jnp.exp(
        jnp.arange(half_dim, dtype=F32) * (-2.0 * math.log(THETA_BASE) / HEAD_SIZE)
    )
    angles = token_position.astype(F32)[:, None] * frequency
    return jnp.cos(angles), jnp.sin(angles)


def apply_rotary(values, cosine, sine):
    half_dim = HEAD_SIZE // 2
    first_half = values[..., :half_dim]
    second_half = values[..., half_dim:]
    return jnp.concatenate(
        [first_half * cosine - second_half * sine, second_half * cosine + first_half * sine],
        axis=-1,
    )


def head_norm_rotary(values, gain, cosine, sine):
    rows, width = values.shape
    heads = values.reshape(rows, width // HEAD_SIZE, HEAD_SIZE)
    turned = apply_rotary(row_scaling(heads, gain), cosine[:, None, :], sine[:, None, :])
    return turned.reshape(rows, width)


def shards(
    span_hidden,
    attn_gain,
    kv_weight,
    q_gain,
    key_norm_gain,
    q_weight,
    o_weight,
    decode_hidden,
    cache,
    cache_len,
    block_owner,
    block_slot,
):
    seq_index = lax.axis_index("z") * Y + lax.axis_index("y")
    prefill_side = lax.axis_index("role") == 0
    span_rows = span_hidden.shape[1]
    local_width = kv_weight.shape[2]
    local_heads = local_width // HEAD_SIZE
    steps, requests, width = decode_hidden.shape
    rows = steps * requests
    local_query = q_weight.shape[1]
    seq_count, block_count = block_owner.shape
    buffer_tokens = seq_count * CAPACITY * BLOCK_TOKENS

    def prefill():
        normed = row_scaling(span_hidden[0].astype(F32), attn_gain).astype(BF16)
        projected = jnp.einsum("td,dcw->ctw", normed, kv_weight, preferred_element_type=F32)
        cosine, sine = rotary_tables(seq_index * span_rows + jnp.arange(span_rows, dtype=jnp.int32))
        keys = head_norm_rotary(projected[0], key_norm_gain, cosine, sine)
        span_kv = jnp.concatenate([keys, projected[1]], axis=1).astype(BF16)

        block_number = jnp.arange(block_count, dtype=jnp.int32)
        same_owner = block_owner[:, :, None] == block_owner[:, None, :]
        earlier = block_number[None, None, :] < block_number[None, :, None]
        rank_table = jnp.sum(jnp.logical_and(same_owner, earlier).astype(jnp.int32), axis=2)
        token = jnp.arange(span_rows, dtype=jnp.int32) % BLOCK_TOKENS
        place = jnp.arange(buffer_tokens, dtype=jnp.int32)
        own_owner = lax.dynamic_index_in_dim(block_owner, seq_index, 0, keepdims=False)
        own_rank = lax.dynamic_index_in_dim(rank_table, seq_index, 0, keepdims=False)
        sent_to = jnp.repeat(own_owner * CAPACITY + own_rank, BLOCK_TOKENS) * BLOCK_TOKENS + token
        spread = (place[:, None] == sent_to[None, :]).astype(BF16)
        payload = jnp.dot(spread, span_kv, preferred_element_type=F32).astype(BF16)
        arrived = lax.all_to_all(
            payload.reshape(seq_count, CAPACITY * BLOCK_TOKENS, 2 * local_width),
            SEQ, split_axis=0, concat_axis=0, tiled=True,
        ).reshape(buffer_tokens, 2 * local_width)
        came_as = jnp.arange(seq_count, dtype=jnp.int32)[:, None] * CAPACITY + rank_table
        target = jnp.where(block_owner == seq_index, block_slot, -1)
        source = jnp.sum(
            jnp.where(target[None] == block_number[:, None, None], came_as[None], 0), axis=(1, 2)
        )
        taken_from = jnp.repeat(source, BLOCK_TOKENS) * BLOCK_TOKENS + token
        gather = (taken_from[:, None] == place[None, :]).astype(BF16)
        pool = jnp.dot(gather, arrived, preferred_element_type=F32).astype(BF16)
        return span_kv, pool, jnp.zeros((steps, requests, width), BF16)

    def decode():
        weight = lax.all_to_all(
            jnp.broadcast_to(q_weight[None], (Y,) + q_weight.shape), "y",
            split_axis=0, concat_axis=0, tiled=True,
        ).reshape(Y * q_weight.shape[0], local_query)
        out_weight = lax.all_to_all(jnp.broadcast_to(o_weight[None], (Y,) + o_weight.shape), "y", split_axis=0, concat_axis=0, tiled=True)
        hidden = decode_hidden.reshape(rows, width).astype(F32)
        normed = row_scaling(hidden, attn_gain).astype(BF16)
        chunk = width // Z
        spread = lax.all_to_all(
            normed.reshape(rows, Z, chunk).transpose(1, 0, 2), "z",
            split_axis=0, concat_axis=0, tiled=True,
        ).reshape(Z * rows, chunk)

        position = (
            cache_len[None, :] + jnp.arange(steps, dtype=jnp.int32)[:, None]
        ).reshape(rows)
        cosine, sine = rotary_tables(position)
        fresh = jnp.einsum("rd,dcw->crw", normed, kv_weight, preferred_element_type=F32)
        new_keys = head_norm_rotary(fresh[0], key_norm_gain, cosine, sine).astype(BF16)
        new_values = fresh[1].astype(BF16)

        partial = jnp.dot(spread, weight, preferred_element_type=F32).astype(BF16)
        returned = lax.all_to_all(
            partial.reshape(Z, rows, local_query), "z", split_axis=0, concat_axis=0, tiled=True
        )
        query_raw = jnp.sum(returned.astype(F32), axis=0)
        query = head_norm_rotary(query_raw, q_gain, cosine, sine).astype(BF16)

        context = cache.shape[1]
        group = local_query // local_width
        scale = HEAD_SIZE ** (-0.5)
        row = jnp.arange(rows, dtype=jnp.int32)
        slot = jnp.arange(requests * context, dtype=jnp.int32)
        limit = jnp.repeat(cache_len, context)
        own = (row[:, None] % requests) == (slot[None, :] // context)
        seen = jnp.logical_and(own, (slot % context)[None, :] < limit[None, :])
        own_new = (row[:, None] % requests) == (row[None, :] % requests)
        seen_new = jnp.logical_and(own_new, row[None, :] // requests <= row[:, None] // requests)
        attended = []
        for head in range(local_heads):
            columns = slice(head * HEAD_SIZE, (head + 1) * HEAD_SIZE)
            keys = cache[:, :, 0, columns].reshape(requests * context, HEAD_SIZE)
            values = cache[:, :, 1, columns].reshape(requests * context, HEAD_SIZE)
            queries = query[:, head * group * HEAD_SIZE : (head + 1) * group * HEAD_SIZE]
            queries = queries.reshape(rows, group, HEAD_SIZE)
            old = jnp.einsum("rgd,kd->rgk", queries, keys, preferred_element_type=F32) * scale
            new = jnp.einsum(
                "rgd,kd->rgk", queries, new_keys[:, columns], preferred_element_type=F32
            ) * scale
            old = jnp.where(seen[:, None, :], old, -jnp.inf)
            new = jnp.where(seen_new[:, None, :], new, -jnp.inf)
            top = jnp.maximum(
                jnp.max(old, axis=-1, keepdims=True), jnp.max(new, axis=-1, keepdims=True)
            )
            old_exp = jnp.exp(old - top)
            new_exp = jnp.exp(new - top)
            total = jnp.sum(old_exp, axis=-1, keepdims=True) + jnp.sum(
                new_exp, axis=-1, keepdims=True
            )
            mixed = jnp.einsum(
                "rgk,kd->rgd", (old_exp / total).astype(BF16), values, preferred_element_type=F32
            ) + jnp.einsum(
                "rgk,kd->rgd", (new_exp / total).astype(BF16), new_values[:, columns],
                preferred_element_type=F32,
            )
            attended.append(mixed.reshape(rows, group * HEAD_SIZE))
        attended = jnp.concatenate(attended, axis=1).astype(BF16)
        gathered = lax.all_to_all(
            jnp.broadcast_to(attended[None], (Z, rows, local_query)), "z",
            split_axis=0, concat_axis=0, tiled=True,
        ).reshape(Z * rows, local_query)
        partial_out = jnp.concatenate(
            [
                jnp.dot(gathered, out_weight[part], preferred_element_type=F32).astype(BF16)
                for part in range(Y)
            ],
            axis=1,
        )
        back = lax.all_to_all(
            partial_out.reshape(Z, rows, chunk), "z", split_axis=0, concat_axis=0, tiled=True
        )
        tp_count = lax.axis_size("tp")
        delta = back.astype(F32)
        for shift in range(1, tp_count):
            route = [(i, (i + shift) % tp_count) for i in range(tp_count)]
            delta = delta + lax.ppermute(back, "tp", route).astype(F32)
        delta = delta.transpose(1, 0, 2).reshape(rows, width)
        decoded = (hidden + delta).astype(BF16).reshape(steps, requests, width)
        nothing = jnp.zeros((span_rows, 2 * local_width), BF16)
        return nothing, nothing, decoded

    span_kv, pool, decoded = lax.cond(prefill_side, prefill, decode)
    handed = lax.ppermute(pool, "role", [(0, 1)])
    kv = jnp.where(prefill_side, span_kv, handed)
    kv_sections = kv.reshape(1, span_rows, 2, local_width)
    return kv_sections, decoded[None]


def solution(mesh):
    shape = mesh.devices.shape
    fine = Mesh(mesh.devices.reshape(shape[0], Z, Y, shape[2]), ("role", "z", "y", "tp"))
    placed = (
        P("role", SEQ, None),
        P(),
        P(None, None, "tp"),
        P(),
        P(),
        P(SEQ, "tp"),
        P("tp", SEQ),
        P(None, SEQ, None),
        P(SEQ, None, None, "tp"),
        P(SEQ),
        P(),
        P(),
    )
    return jax.shard_map(
        shards,
        mesh=fine,
        in_specs=placed,
        out_specs=(P("role", SEQ, None, "tp"), P("role", None, SEQ, None)),
        check_vma=False,
    )
```

```python
import math

import jax
import jax.numpy as jnp
from jax import lax
from jax.experimental import pallas as pl
from jax.experimental.pallas import tpu as pltpu
from jax.sharding import Mesh, PartitionSpec as P

QUERY_HEADS = 64
KEY_VALUE_HEADS = 8
HEAD_SIZE = 128
EPSILON = 1e-06
THETA_BASE = 1000000.0

Z, Y = 8, 4
SEQ = ("z", "y")
BLOCK_TOKENS = 8
CAPACITY = 2
VMEM_LIMIT = 32 * 2**20
F32, BF16 = jnp.float32, jnp.bfloat16


def row_scaling(values, weights):
    return values * lax.rsqrt(jnp.mean(values * values, axis=-1, keepdims=True) + EPSILON) * weights


def rotary_tables(token_position):
    half_dim = HEAD_SIZE // 2
    frequency = jnp.exp(
        jnp.arange(half_dim, dtype=F32) * (-2.0 * math.log(THETA_BASE) / HEAD_SIZE)
    )
    angles = token_position.astype(F32)[:, None] * frequency
    return jnp.cos(angles), jnp.sin(angles)


def apply_rotary(values, cosine, sine):
    half_dim = HEAD_SIZE // 2
    first_half = values[..., :half_dim]
    second_half = values[..., half_dim:]
    return jnp.concatenate(
        [first_half * cosine - second_half * sine, second_half * cosine + first_half * sine],
        axis=-1,
    )


def head_norm_rotary(values, gain, cosine, sine):
    rows, width = values.shape
    heads = values.reshape(rows, width // HEAD_SIZE, HEAD_SIZE)
    turned = apply_rotary(row_scaling(heads, gain), cosine[:, None, :], sine[:, None, :])
    return turned.reshape(rows, width)


def dot(a, b):
    return jnp.dot(a, b, preferred_element_type=F32)


def norm_kernel(y_ref, hidden_ref, gain_ref, spread_ref, normed_ref, *unused):
    hidden = jnp.concatenate(
        [hidden_ref[step].astype(F32) for step in range(hidden_ref.shape[0])], axis=0
    )
    normed = row_scaling(hidden, gain_ref[...])
    normed_ref[...] = normed.astype(BF16)
    chunk = spread_ref.shape[2]
    shift = lax.rem(Y - y_ref[0], Y) * (chunk // Y)
    for z in range(Z):
        block = normed[:, z * chunk : (z + 1) * chunk]
        spread_ref[z] = pltpu.roll(block, shift, axis=1).astype(BF16)


def query_kernel(rows_ref, own_ref, first_ref, second_ref, third_ref, out_ref):
    tile = 512
    for start in range(0, out_ref.shape[1], tile):
        columns = slice(start, start + tile)
        weight = jnp.concatenate(
            [ref[:, columns] for ref in (own_ref, first_ref, second_ref, third_ref)], axis=0
        )
        out_ref[:, columns] = dot(rows_ref[...], weight).astype(BF16)


def attention_kernel(
    length_ref,
    returned_ref,
    gain_ref,
    cosine_ref,
    sine_ref,
    keys_ref,
    values_ref,
    new_keys_ref,
    new_values_ref,
    out_ref,
    *unused,
):
    rows = returned_ref.shape[1]
    requests = rows // 4
    slots, local_width = keys_ref.shape
    context = slots // requests
    group = returned_ref.shape[2] // local_width
    scale = HEAD_SIZE ** (-0.5)
    cosine = jnp.concatenate([cosine_ref[...]] * group, axis=0)
    sine = jnp.concatenate([sine_ref[...]] * group, axis=0)

    def indices(columns):
        row = lax.broadcasted_iota(jnp.int32, (group * rows, columns), 0) % rows
        return row, lax.broadcasted_iota(jnp.int32, (group * rows, columns), 1)

    row, slot = indices(slots)
    request = slot // context
    limit = jnp.full_like(slot, length_ref[0])
    for one in range(1, requests):
        limit = jnp.where(request == one, length_ref[one], limit)
    seen = jnp.logical_and(row % requests == request, slot % context < limit)
    row, new = indices(rows)
    seen_new = jnp.logical_and(
        row % requests == new % requests, new // requests <= row // requests
    )
    for head in range(local_width // HEAD_SIZE):
        columns = slice(head * HEAD_SIZE, (head + 1) * HEAD_SIZE)
        query = []
        for one in range(head * group, (head + 1) * group):
            part = slice(one * HEAD_SIZE, (one + 1) * HEAD_SIZE)
            total = returned_ref[0, :, part].astype(F32)
            for z in range(1, Z):
                total += returned_ref[z, :, part].astype(F32)
            query.append(total)
        query = row_scaling(jnp.concatenate(query, axis=0), gain_ref[...])
        query = query * cosine + pltpu.roll(query, HEAD_SIZE // 2, axis=1) * sine
        query = query.astype(BF16)
        transposed = (((1,), (1,)), ((), ()))
        old = lax.dot_general(
            query, keys_ref[:, columns], transposed, preferred_element_type=F32
        ) * scale
        new = lax.dot_general(
            query, new_keys_ref[:, columns], transposed, preferred_element_type=F32
        ) * scale
        old = jnp.where(seen, old, -jnp.inf)
        new = jnp.where(seen_new, new, -jnp.inf)
        top = jnp.maximum(
            jnp.max(old, axis=-1, keepdims=True), jnp.max(new, axis=-1, keepdims=True)
        )
        old_exp = jnp.exp(old - top)
        new_exp = jnp.exp(new - top)
        total = jnp.sum(old_exp, axis=-1, keepdims=True) + jnp.sum(new_exp, axis=-1, keepdims=True)
        mixed = dot((old_exp / total).astype(BF16), values_ref[:, columns])
        mixed += dot((new_exp / total).astype(BF16), new_values_ref[:, columns])
        mixed = mixed.astype(BF16)
        for one in range(group):
            part = head * group + one
            block = mixed[one * rows : (one + 1) * rows]
            for z in range(Z):
                out_ref[z, :, part * HEAD_SIZE : (part + 1) * HEAD_SIZE] = block


def shards(
    span_hidden,
    attn_gain,
    kv_weight,
    q_gain,
    key_norm_gain,
    q_weight,
    o_weight,
    decode_hidden,
    cache,
    cache_len,
    block_owner,
    block_slot,
):
    y_index = lax.axis_index("y")
    seq_index = lax.axis_index("z") * Y + y_index
    prefill_side = lax.axis_index("role") == 0
    span_rows = span_hidden.shape[1]
    local_width = kv_weight.shape[2]
    steps, requests, width = decode_hidden.shape
    rows = steps * requests
    depth, local_query = q_weight.shape
    out_depth, out_width = o_weight.shape
    seq_count, block_count = block_owner.shape
    buffer_tokens = seq_count * CAPACITY * BLOCK_TOKENS
    chunk = width // Z
    context = cache.shape[1]
    exchanged = (Z, rows, local_query)

    whole = pl.BlockSpec(memory_space=pltpu.VMEM)
    unwritten = pl.BlockSpec(memory_space=pl.ANY)
    section = jax.ShapeDtypeStruct((span_rows, 2, local_width), BF16)
    buffer = jax.ShapeDtypeStruct((seq_count, CAPACITY * BLOCK_TOKENS, 2 * local_width), BF16)

    def rank_table():
        block_number = jnp.arange(block_count, dtype=jnp.int32)
        same_owner = block_owner[:, :, None] == block_owner[:, None, :]
        earlier = block_number[None, None, :] < block_number[None, :, None]
        return jnp.sum(jnp.logical_and(same_owner, earlier).astype(jnp.int32), axis=2)

    token = jnp.arange(span_rows, dtype=jnp.int32) % BLOCK_TOKENS
    place = jnp.arange(buffer_tokens, dtype=jnp.int32)

    def prefill(*_):
        normed = row_scaling(span_hidden[0].astype(F32), attn_gain).astype(BF16)
        projected = jnp.einsum("td,dcw->ctw", normed, kv_weight, preferred_element_type=F32)
        cosine, sine = rotary_tables(seq_index * span_rows + jnp.arange(span_rows, dtype=jnp.int32))
        keys = head_norm_rotary(projected[0], key_norm_gain, cosine, sine)
        span_kv = jnp.concatenate([keys, projected[1]], axis=1).astype(BF16)
        own_owner = lax.dynamic_index_in_dim(block_owner, seq_index, 0, keepdims=False)
        own_rank = lax.dynamic_index_in_dim(rank_table(), seq_index, 0, keepdims=False)
        sent_to = jnp.repeat(own_owner * CAPACITY + own_rank, BLOCK_TOKENS) * BLOCK_TOKENS + token
        spread = (place[:, None] == sent_to[None, :]).astype(BF16)
        payload = dot(spread, span_kv).astype(BF16)
        return (
            jnp.zeros((Z * rows, chunk), BF16),
            jnp.zeros((rows, HEAD_SIZE), F32),
            jnp.zeros((rows, HEAD_SIZE), F32),
            jnp.zeros((rows, local_width), BF16),
            jnp.zeros((rows, local_width), BF16),
            span_kv.reshape(section.shape),
            payload.reshape(buffer.shape),
        )

    def route(payload, *_):
        turned = o_weight.T
        out_weight = jnp.zeros((Y, out_width, out_depth), BF16)
        for shift in range(Y):
            part = turned
            if shift > 0:
                part = lax.ppermute(turned, "y", [(i, (i - shift) % Y) for i in range(Y)])
            out_weight = lax.dynamic_update_index_in_dim(
                out_weight, part, lax.rem(y_index + shift, Y), 0
            )
        arrived = lax.all_to_all(payload, SEQ, split_axis=0, concat_axis=0, tiled=True)
        block_number = jnp.arange(block_count, dtype=jnp.int32)
        came_as = jnp.arange(seq_count, dtype=jnp.int32)[:, None] * CAPACITY + rank_table()
        target = jnp.where(block_owner == seq_index, block_slot, -1)
        source = jnp.sum(
            jnp.where(target[None] == block_number[:, None, None], came_as[None], 0), axis=(1, 2)
        )
        taken_from = jnp.repeat(source, BLOCK_TOKENS) * BLOCK_TOKENS + token
        gather = (taken_from[:, None] == place[None, :]).astype(BF16)
        pool = dot(gather, arrived.reshape(buffer_tokens, 2 * local_width)).astype(BF16)
        return (
            pool.reshape(section.shape),
            out_weight.reshape(Y * out_width, out_depth),
            jnp.zeros(exchanged, BF16),
        )

    arrived_weights = []
    for shift in range(1, Y):
        pairs = [(i, Y + (i - shift) % Y) for i in range(Y)]
        arrived_weights.append(lax.ppermute(q_weight, ("role", "y"), pairs))

    def project(*_):
        spread, normed, span_kv, payload = pl.pallas_call(
            norm_kernel,
            out_shape=(
                jax.ShapeDtypeStruct((Z, rows, chunk), BF16),
                jax.ShapeDtypeStruct((rows, width), BF16),
                section,
                buffer,
            ),
            in_specs=[
                pl.BlockSpec(memory_space=pltpu.SMEM),
                whole,
                whole,
            ],
            out_specs=[whole] * 2 + [unwritten] * 2,
        )(y_index.astype(jnp.int32).reshape(1), decode_hidden, attn_gain.reshape(1, width))
        spread = lax.all_to_all(spread, "z", split_axis=0, concat_axis=0, tiled=True)
        position = (
            cache_len[None, :] + jnp.arange(steps, dtype=jnp.int32)[:, None]
        ).reshape(rows)
        cosine, sine = rotary_tables(position)
        fresh = jnp.einsum("rd,dcw->crw", normed, kv_weight, preferred_element_type=F32)
        new_keys = head_norm_rotary(fresh[0], key_norm_gain, cosine, sine).astype(BF16)
        new_values = fresh[1].astype(BF16)
        cosine = jnp.concatenate([cosine, cosine], axis=1)
        sine = jnp.concatenate([-sine, sine], axis=1)
        spread = spread.reshape(Z * rows, chunk)
        return spread, cosine, sine, new_keys, new_values, span_kv, payload

    spread, cosine, sine, new_keys, new_values, span_kv, payload = lax.cond(
        prefill_side, prefill, project
    )

    def attend(payload, spread, cosine, sine, new_keys, new_values, *weights):
        partial = pl.pallas_call(
            query_kernel,
            in_specs=[whole] * 5,
            out_specs=whole,
            out_shape=jax.ShapeDtypeStruct((Z * rows, local_query), BF16),
            compiler_params=pltpu.CompilerParams(vmem_limit_bytes=VMEM_LIMIT),
        )(spread, q_weight, *weights)
        returned = lax.all_to_all(
            partial.reshape(exchanged), "z", split_axis=0, concat_axis=0, tiled=True
        )
        slots = requests * context
        attended, pool, out_weight = pl.pallas_call(
            attention_kernel,
            out_shape=(
                jax.ShapeDtypeStruct(exchanged, BF16),
                section,
                jax.ShapeDtypeStruct((Y * out_width, out_depth), BF16),
            ),
            in_specs=[pl.BlockSpec(memory_space=pltpu.SMEM)] + [whole] * 8,
            out_specs=[whole] + [unwritten] * 2,
            compiler_params=pltpu.CompilerParams(vmem_limit_bytes=VMEM_LIMIT),
        )(
            cache_len,
            returned,
            q_gain.reshape(1, HEAD_SIZE),
            cosine,
            sine,
            cache[:, :, 0].reshape(slots, local_width),
            cache[:, :, 1].reshape(slots, local_width),
            new_keys,
            new_values,
        )
        return pool, out_weight, attended

    pool, out_weight, attended = lax.cond(
        prefill_side, route, attend,
        payload, spread, cosine, sine, new_keys, new_values, *arrived_weights,
    )
    out_weight = lax.ppermute(out_weight, "role", [(0, 1)])
    pool = lax.ppermute(pool, "role", [(0, 1)])

    def gather(attended):
        return lax.all_to_all(attended, "z", split_axis=0, concat_axis=0, tiled=True)

    attended = lax.cond(prefill_side, lambda attended: attended, gather, attended)

    def finish(attended, out_weight):
        partial = lax.dot_general(
            attended.reshape(Z * rows, local_query),
            out_weight,
            (((1,), (1,)), ((), ())),
            preferred_element_type=F32,
        ).astype(BF16)
        back = lax.all_to_all(
            partial.reshape(Z, rows, chunk), "z", split_axis=0, concat_axis=0, tiled=True
        )
        tp_count = lax.axis_size("tp")
        delta = back.astype(F32)
        for shift in range(1, tp_count):
            pairs = [(i, (i + shift) % tp_count) for i in range(tp_count)]
            delta = delta + lax.ppermute(back, "tp", pairs).astype(F32)
        delta = delta.transpose(1, 0, 2).reshape(steps, requests, width)
        return (decode_hidden.astype(F32) + delta).astype(BF16)[None]

    def idle_finish(attended, out_weight):
        return jnp.zeros((1, steps, requests, width), BF16)

    decoded = lax.cond(prefill_side, idle_finish, finish, attended, out_weight)
    return jnp.where(prefill_side, span_kv, pool)[None], decoded


def solution(mesh):
    shape = mesh.devices.shape
    fine = Mesh(mesh.devices.reshape(shape[0], Z, Y, shape[2]), ("role", "z", "y", "tp"))
    placed = (
        P("role", SEQ, None),
        P(),
        P(None, None, "tp"),
        P(),
        P(),
        P(SEQ, "tp"),
        P("tp", SEQ),
        P(None, SEQ, None),
        P(SEQ, None, None, "tp"),
        P(SEQ),
        P(),
        P(),
    )
    return jax.shard_map(
        shards,
        mesh=fine,
        in_specs=placed,
        out_specs=(P("role", SEQ, None, "tp"), P("role", None, SEQ, None)),
        check_vma=False,
    )
```

```python
import math

import jax
import jax.numpy as jnp
from jax import lax
from jax.experimental import pallas as pl
from jax.experimental.pallas import tpu as pltpu
from jax.sharding import Mesh, PartitionSpec as P

QUERY_HEADS = 64
KEY_VALUE_HEADS = 8
HEAD_SIZE = 128
EPSILON = 1e-06
THETA_BASE = 1000000.0

Z, Y = 8, 4
SEQ = ("z", "y")
BLOCK_TOKENS = 8
CAPACITY = 2
VMEM_LIMIT = 32 * 2**20
F32, BF16 = jnp.float32, jnp.bfloat16


def row_scaling(values, weights):
    return values * lax.rsqrt(jnp.mean(values * values, axis=-1, keepdims=True) + EPSILON) * weights


def rotary_tables(token_position):
    half_dim = HEAD_SIZE // 2
    frequency = jnp.exp(
        jnp.arange(half_dim, dtype=F32) * (-2.0 * math.log(THETA_BASE) / HEAD_SIZE)
    )
    angles = token_position.astype(F32)[:, None] * frequency
    return jnp.cos(angles), jnp.sin(angles)


def apply_rotary(values, cosine, sine):
    half_dim = HEAD_SIZE // 2
    first_half = values[..., :half_dim]
    second_half = values[..., half_dim:]
    return jnp.concatenate(
        [first_half * cosine - second_half * sine, second_half * cosine + first_half * sine],
        axis=-1,
    )


def head_norm_rotary(values, gain, cosine, sine):
    rows, width = values.shape
    heads = values.reshape(rows, width // HEAD_SIZE, HEAD_SIZE)
    turned = apply_rotary(row_scaling(heads, gain), cosine[:, None, :], sine[:, None, :])
    return turned.reshape(rows, width)


def dot(a, b):
    return jnp.dot(a, b, preferred_element_type=F32)


def norm_kernel(y_ref, hidden_ref, gain_ref, spread_ref, normed_ref, *unused):
    hidden = jnp.concatenate(
        [hidden_ref[step].astype(F32) for step in range(hidden_ref.shape[0])], axis=0
    )
    normed = row_scaling(hidden, gain_ref[...])
    normed_ref[...] = normed.astype(BF16)
    chunk = spread_ref.shape[2]
    shift = lax.rem(Y - y_ref[0], Y) * (chunk // Y)
    for z in range(Z):
        block = normed[:, z * chunk : (z + 1) * chunk]
        spread_ref[z] = pltpu.roll(block, shift, axis=1).astype(BF16)


def query_kernel(rows_ref, own_ref, first_ref, second_ref, third_ref, out_ref):
    tile = 512
    for start in range(0, out_ref.shape[1], tile):
        columns = slice(start, start + tile)
        weight = jnp.concatenate(
            [ref[:, columns] for ref in (own_ref, first_ref, second_ref, third_ref)], axis=0
        )
        out_ref[:, columns] = dot(rows_ref[...], weight).astype(BF16)


def attention_kernel(
    length_ref,
    returned_ref,
    gain_ref,
    cosine_ref,
    sine_ref,
    keys_ref,
    values_ref,
    new_keys_ref,
    new_values_ref,
    out_ref,
    *unused,
):
    rows = returned_ref.shape[1]
    requests = rows // 4
    slots, local_width = keys_ref.shape
    context = slots // requests
    group = returned_ref.shape[2] // local_width
    scale = HEAD_SIZE ** (-0.5)
    cosine = jnp.concatenate([cosine_ref[...]] * group, axis=0)
    sine = jnp.concatenate([sine_ref[...]] * group, axis=0)

    def indices(columns):
        row = lax.broadcasted_iota(jnp.int32, (group * rows, columns), 0) % rows
        return row, lax.broadcasted_iota(jnp.int32, (group * rows, columns), 1)

    row, slot = indices(slots)
    request = slot // context
    limit = jnp.full_like(slot, length_ref[0])
    for one in range(1, requests):
        limit = jnp.where(request == one, length_ref[one], limit)
    seen = jnp.logical_and(row % requests == request, slot % context < limit)
    row, new = indices(rows)
    seen_new = jnp.logical_and(
        row % requests == new % requests, new // requests <= row // requests
    )
    for head in range(local_width // HEAD_SIZE):
        columns = slice(head * HEAD_SIZE, (head + 1) * HEAD_SIZE)
        query = []
        for one in range(head * group, (head + 1) * group):
            part = slice(one * HEAD_SIZE, (one + 1) * HEAD_SIZE)
            total = returned_ref[0, :, part].astype(F32)
            for z in range(1, Z):
                total += returned_ref[z, :, part].astype(F32)
            query.append(total)
        query = row_scaling(jnp.concatenate(query, axis=0), gain_ref[...])
        query = query * cosine + pltpu.roll(query, HEAD_SIZE // 2, axis=1) * sine
        query = query.astype(BF16)
        transposed = (((1,), (1,)), ((), ()))
        old = lax.dot_general(
            query, keys_ref[:, columns], transposed, preferred_element_type=F32
        ) * scale
        new = lax.dot_general(
            query, new_keys_ref[:, columns], transposed, preferred_element_type=F32
        ) * scale
        old = jnp.where(seen, old, -jnp.inf)
        new = jnp.where(seen_new, new, -jnp.inf)
        top = jnp.maximum(
            jnp.max(old, axis=-1, keepdims=True), jnp.max(new, axis=-1, keepdims=True)
        )
        old_exp = jnp.exp(old - top)
        new_exp = jnp.exp(new - top)
        total = jnp.sum(old_exp, axis=-1, keepdims=True) + jnp.sum(new_exp, axis=-1, keepdims=True)
        mixed = dot((old_exp / total).astype(BF16), values_ref[:, columns])
        mixed += dot((new_exp / total).astype(BF16), new_values_ref[:, columns])
        mixed = mixed.astype(BF16)
        for one in range(group):
            part = head * group + one
            block = mixed[one * rows : (one + 1) * rows]
            for z in range(Z):
                out_ref[z, :, part * HEAD_SIZE : (part + 1) * HEAD_SIZE] = block


def copy_kernel(source_ref, out_ref):
    out_ref[0] = source_ref[...]


def packed(pool, width):
    sides = width // pool.shape[1]
    run = pool.shape[0] // sides
    return jnp.concatenate([pool[i * run : (i + 1) * run] for i in range(sides)], axis=1)


def base_kernel(hidden_ref, back_ref, out_ref):
    chunk = back_ref.shape[2]
    for z in range(Z):
        columns = slice(z * chunk, (z + 1) * chunk)
        hidden = jnp.concatenate(
            [hidden_ref[step, :, columns].astype(F32) for step in range(hidden_ref.shape[0])],
            axis=0,
        )
        out_ref[z] = hidden + back_ref[z].astype(F32)


def sum_kernel(base_ref, first_ref, second_ref, third_ref, out_ref):
    steps, requests = out_ref.shape[1:3]
    chunk = base_ref.shape[2]
    for z in range(Z):
        total = base_ref[z] + (
            first_ref[z].astype(F32) + second_ref[z].astype(F32) + third_ref[z].astype(F32)
        )
        total = total.astype(BF16)
        for step in range(steps):
            out_ref[0, step, :, z * chunk : (z + 1) * chunk] = total[
                step * requests : (step + 1) * requests
            ]


def unpack_kernel(handed_ref, out_ref):
    tokens, sections, width = out_ref.shape[1:]
    sides = handed_ref.shape[1] // (sections * width)
    run = tokens // sides
    for i in range(sides):
        for section in range(sections):
            start = (i * sections + section) * width
            out_ref[0, i * run : (i + 1) * run, section, :] = handed_ref[:, start : start + width]


def shards(
    span_hidden,
    attn_gain,
    kv_weight,
    q_gain,
    key_norm_gain,
    q_weight,
    o_weight,
    decode_hidden,
    cache,
    cache_len,
    block_owner,
    block_slot,
):
    y_index = lax.axis_index("y")
    seq_index = lax.axis_index("z") * Y + y_index
    prefill_side = lax.axis_index("role") == 0
    span_rows = span_hidden.shape[1]
    local_width = kv_weight.shape[2]
    steps, requests, width = decode_hidden.shape
    rows = steps * requests
    depth, local_query = q_weight.shape
    out_depth, out_width = o_weight.shape
    seq_count, block_count = block_owner.shape
    buffer_tokens = seq_count * CAPACITY * BLOCK_TOKENS
    chunk = width // Z
    context = cache.shape[1]
    slots = requests * context
    exchanged = (Z, rows, local_query)

    whole = pl.BlockSpec(memory_space=pltpu.VMEM)
    unwritten = pl.BlockSpec(memory_space=pl.ANY)
    section = jax.ShapeDtypeStruct((span_rows, 2, local_width), BF16)
    buffer = jax.ShapeDtypeStruct((seq_count, CAPACITY * BLOCK_TOKENS, 2 * local_width), BF16)

    def rank_table():
        block_number = jnp.arange(block_count, dtype=jnp.int32)
        same_owner = block_owner[:, :, None] == block_owner[:, None, :]
        earlier = block_number[None, None, :] < block_number[None, :, None]
        return jnp.sum(jnp.logical_and(same_owner, earlier).astype(jnp.int32), axis=2)

    pool_rows = span_rows * 2 * local_width // out_depth
    handed_over = jax.ShapeDtypeStruct((Y * out_width + pool_rows, out_depth), BF16)

    def one_hot(blocks):
        token = lax.broadcasted_iota(jnp.int32, (block_count, BLOCK_TOKENS), 1)
        at = (blocks[:, None] * BLOCK_TOKENS + token).reshape(1, span_rows)
        place = lax.broadcasted_iota(jnp.int32, (buffer_tokens, span_rows), 0)
        return (place == at).astype(BF16)

    def prefill(*_):
        normed = row_scaling(span_hidden[0].astype(F32), attn_gain).astype(BF16)
        projected = jnp.einsum("td,dcw->ctw", normed, kv_weight, preferred_element_type=F32)
        cosine, sine = rotary_tables(seq_index * span_rows + jnp.arange(span_rows, dtype=jnp.int32))
        keys = head_norm_rotary(projected[0], key_norm_gain, cosine, sine)
        span_kv = jnp.concatenate([keys, projected[1]], axis=1).astype(BF16)
        own_owner = lax.dynamic_index_in_dim(block_owner, seq_index, 0, keepdims=False)
        own_rank = lax.dynamic_index_in_dim(rank_table(), seq_index, 0, keepdims=False)
        payload = dot(one_hot(own_owner * CAPACITY + own_rank), span_kv).astype(BF16)
        return (
            jnp.zeros((Z * rows, chunk), BF16),
            jnp.zeros((rows, HEAD_SIZE), F32),
            jnp.zeros((rows, HEAD_SIZE), F32),
            jnp.zeros((rows, local_width), BF16),
            jnp.zeros((rows, local_width), BF16),
            jnp.zeros((slots, local_width), BF16),
            jnp.zeros((slots, local_width), BF16),
            span_kv.reshape(section.shape),
            payload.reshape(buffer.shape),
        )

    def route(payload, *_):
        turned = o_weight.T
        handed = jnp.zeros(handed_over.shape, BF16)
        for shift in range(Y):
            part = turned
            if shift > 0:
                part = lax.ppermute(turned, "y", [(i, (i - shift) % Y) for i in range(Y)])
            handed = lax.dynamic_update_slice(
                handed, part, (lax.rem(y_index + shift, Y) * out_width, 0)
            )
        arrived = lax.all_to_all(payload, SEQ, split_axis=0, concat_axis=0, tiled=True)
        block_number = jnp.arange(block_count, dtype=jnp.int32)
        came_as = jnp.arange(seq_count, dtype=jnp.int32)[:, None] * CAPACITY + rank_table()
        target = jnp.where(block_owner == seq_index, block_slot, -1)
        source = jnp.sum(
            jnp.where(target[None] == block_number[:, None, None], came_as[None], 0), axis=(1, 2)
        )
        pool = lax.dot_general(
            one_hot(source),
            arrived.reshape(buffer_tokens, 2 * local_width),
            (((0,), (0,)), ((), ())),
            preferred_element_type=F32,
        ).astype(BF16)
        handed = lax.dynamic_update_slice(handed, packed(pool, out_depth), (Y * out_width, 0))
        return handed, jnp.zeros(exchanged, BF16)

    arrived_weights = []
    for shift in range(1, Y):
        pairs = [(i, Y + (i - shift) % Y) for i in range(Y)] + [(Y + i, i) for i in range(Y)]
        arrived_weights.append(lax.ppermute(q_weight, ("role", "y"), pairs))

    def project(*_):
        spread, normed, span_kv, payload = pl.pallas_call(
            norm_kernel,
            out_shape=(
                jax.ShapeDtypeStruct((Z, rows, chunk), BF16),
                jax.ShapeDtypeStruct((rows, width), BF16),
                section,
                buffer,
            ),
            in_specs=[
                pl.BlockSpec(memory_space=pltpu.SMEM),
                whole,
                whole,
            ],
            out_specs=[whole] * 2 + [unwritten] * 2,
        )(y_index.astype(jnp.int32).reshape(1), decode_hidden, attn_gain.reshape(1, width))
        spread = lax.all_to_all(spread, "z", split_axis=0, concat_axis=0, tiled=True)
        position = (
            cache_len[None, :] + jnp.arange(steps, dtype=jnp.int32)[:, None]
        ).reshape(rows)
        cosine, sine = rotary_tables(position)
        fresh = jnp.einsum("rd,dcw->crw", normed, kv_weight, preferred_element_type=F32)
        new_keys = head_norm_rotary(fresh[0], key_norm_gain, cosine, sine).astype(BF16)
        new_values = fresh[1].astype(BF16)
        cosine = jnp.concatenate([cosine, cosine], axis=1)
        sine = jnp.concatenate([-sine, sine], axis=1)
        spread = spread.reshape(Z * rows, chunk)
        keys = cache[:, :, 0].reshape(slots, local_width)
        values = cache[:, :, 1].reshape(slots, local_width)
        return spread, cosine, sine, new_keys, new_values, keys, values, span_kv, payload

    spread, *beside, span_kv, payload = lax.cond(prefill_side, prefill, project)

    def attend(payload, spread, cosine, sine, new_keys, new_values, keys, values, *weights):
        partial = pl.pallas_call(
            query_kernel,
            in_specs=[whole] * 5,
            out_specs=whole,
            out_shape=jax.ShapeDtypeStruct((Z * rows, local_query), BF16),
            compiler_params=pltpu.CompilerParams(vmem_limit_bytes=VMEM_LIMIT),
        )(spread, q_weight, *weights)
        returned = lax.all_to_all(
            partial.reshape(exchanged), "z", split_axis=0, concat_axis=0, tiled=True
        )
        attended, handed = pl.pallas_call(
            attention_kernel,
            out_shape=(
                jax.ShapeDtypeStruct(exchanged, BF16),
                handed_over,
            ),
            in_specs=[pl.BlockSpec(memory_space=pltpu.SMEM)] + [whole] * 8,
            out_specs=[whole, unwritten],
            compiler_params=pltpu.CompilerParams(vmem_limit_bytes=VMEM_LIMIT),
        )(
            cache_len,
            returned,
            q_gain.reshape(1, HEAD_SIZE),
            cosine,
            sine,
            keys,
            values,
            new_keys,
            new_values,
        )
        return handed, attended

    handed, attended = lax.cond(
        prefill_side, route, attend,
        payload, spread, *beside, *arrived_weights,
    )
    handed = lax.ppermute(handed, "role", [(0, 1)])

    def gather(attended):
        return lax.all_to_all(attended, "z", split_axis=0, concat_axis=0, tiled=True)

    attended = lax.cond(prefill_side, lambda attended: attended, gather, attended)

    def placed(kernel, source, block, index):
        return pl.pallas_call(
            kernel,
            grid=(1,),
            in_specs=[pl.BlockSpec(block, lambda i: index)],
            out_specs=pl.BlockSpec((1,) + section.shape, lambda i: (0, 0, 0, 0)),
            out_shape=jax.ShapeDtypeStruct((1,) + section.shape, BF16),
        )(source)

    def finish(attended, span_kv, handed):
        partial = lax.dot_general(
            attended.reshape(Z * rows, local_query),
            handed,
            (((1,), (1,)), ((), ())),
            preferred_element_type=F32,
        )[:, : Y * out_width].astype(BF16)
        back = lax.all_to_all(
            partial.reshape(Z, rows, chunk), "z", split_axis=0, concat_axis=0, tiled=True
        )
        tp_count = lax.axis_size("tp")
        others = []
        for shift in range(1, tp_count):
            pairs = [(i, (i + shift) % tp_count) for i in range(tp_count)]
            others.append(lax.ppermute(back, "tp", pairs))
        base = pl.pallas_call(
            base_kernel,
            in_specs=[whole] * 2,
            out_specs=whole,
            out_shape=jax.ShapeDtypeStruct((Z, rows, chunk), F32),
        )(decode_hidden, back)
        decoded = pl.pallas_call(
            sum_kernel,
            in_specs=[whole] * (1 + len(others)),
            out_specs=whole,
            out_shape=jax.ShapeDtypeStruct((1, steps, requests, width), BF16),
        )(base, *others)
        pool = placed(
            unpack_kernel, handed, (pool_rows, out_depth), (Y * out_width // pool_rows, 0)
        )
        return pool, decoded

    def idle_finish(attended, span_kv, handed):
        return placed(copy_kernel, span_kv, section.shape, (0, 0, 0)), jnp.zeros((1, steps, requests, width), BF16)

    return lax.cond(prefill_side, idle_finish, finish, attended, span_kv, handed)


def solution(mesh):
    shape = mesh.devices.shape
    fine = Mesh(mesh.devices.reshape(shape[0], Z, Y, shape[2]), ("role", "z", "y", "tp"))
    placed = (
        P("role", SEQ, None),
        P(),
        P(None, None, "tp"),
        P(),
        P(),
        P(SEQ, "tp"),
        P("tp", SEQ),
        P(None, SEQ, None),
        P(SEQ, None, None, "tp"),
        P(SEQ),
        P(),
        P(),
    )
    return jax.shard_map(
        shards,
        mesh=fine,
        in_specs=placed,
        out_specs=(P("role", SEQ, None, "tp"), P("role", None, SEQ, None)),
        check_vma=False,
    )
```

```python
import math

import jax
import jax.numpy as jnp
from jax import lax
from jax.experimental import pallas as pl
from jax.experimental.pallas import tpu as pltpu
from jax.sharding import Mesh, PartitionSpec as P

QUERY_HEADS = 64
KEY_VALUE_HEADS = 8
HEAD_SIZE = 128
EPSILON = 1e-06
THETA_BASE = 1000000.0

Z, Y = 8, 4
SEQ = ("z", "y")
BLOCK_TOKENS = 8
CAPACITY = 2
VMEM_LIMIT = 8 * 2**20
F32, BF16 = jnp.float32, jnp.bfloat16


def row_scaling(values, weights):
    return values * lax.rsqrt(jnp.mean(values * values, axis=-1, keepdims=True) + EPSILON) * weights


def rotary_tables(token_position):
    half_dim = HEAD_SIZE // 2
    frequency = jnp.exp(
        jnp.arange(half_dim, dtype=F32) * (-2.0 * math.log(THETA_BASE) / HEAD_SIZE)
    )
    angles = token_position.astype(F32)[:, None] * frequency
    return jnp.cos(angles), jnp.sin(angles)


def apply_rotary(values, cosine, sine):
    half_dim = HEAD_SIZE // 2
    first_half = values[..., :half_dim]
    second_half = values[..., half_dim:]
    return jnp.concatenate(
        [first_half * cosine - second_half * sine, second_half * cosine + first_half * sine],
        axis=-1,
    )


def head_norm_rotary(values, gain, cosine, sine):
    rows, width = values.shape
    heads = values.reshape(rows, width // HEAD_SIZE, HEAD_SIZE)
    turned = apply_rotary(row_scaling(heads, gain), cosine[:, None, :], sine[:, None, :])
    return turned.reshape(rows, width)


def dot(a, b):
    return jnp.dot(a, b, preferred_element_type=F32)


def norm_kernel(y_ref, hidden_ref, gain_ref, spread_ref, normed_ref, *unused):
    hidden = jnp.concatenate(
        [hidden_ref[step].astype(F32) for step in range(hidden_ref.shape[0])], axis=0
    )
    normed = row_scaling(hidden, gain_ref[...])
    normed_ref[...] = normed.astype(BF16)
    chunk = spread_ref.shape[2]
    shift = lax.rem(Y - y_ref[0], Y) * (chunk // Y)
    for z in range(Z):
        block = normed[:, z * chunk : (z + 1) * chunk]
        spread_ref[z] = pltpu.roll(block, shift, axis=1).astype(BF16)


def query_kernel(rows_ref, own_ref, first_ref, second_ref, third_ref, out_ref):
    tile = 512
    for start in range(0, out_ref.shape[1], tile):
        columns = slice(start, start + tile)
        weight = jnp.concatenate(
            [ref[:, columns] for ref in (own_ref, first_ref, second_ref, third_ref)], axis=0
        )
        out_ref[:, columns] = dot(rows_ref[...], weight).astype(BF16)


def attention_kernel(
    length_ref,
    returned_ref,
    gain_ref,
    cosine_ref,
    sine_ref,
    keys_ref,
    values_ref,
    new_keys_ref,
    new_values_ref,
    out_ref,
    *unused,
):
    rows = returned_ref.shape[1]
    requests = rows // 4
    slots, local_width = keys_ref.shape
    context = slots // requests
    group = returned_ref.shape[2] // local_width
    scale = HEAD_SIZE ** (-0.5)
    cosine = jnp.concatenate([cosine_ref[...]] * group, axis=0)
    sine = jnp.concatenate([sine_ref[...]] * group, axis=0)

    def indices(columns):
        row = lax.broadcasted_iota(jnp.int32, (group * rows, columns), 0) % rows
        return row, lax.broadcasted_iota(jnp.int32, (group * rows, columns), 1)

    row, slot = indices(slots)
    request = slot // context
    limit = jnp.full_like(slot, length_ref[0])
    for one in range(1, requests):
        limit = jnp.where(request == one, length_ref[one], limit)
    seen = jnp.logical_and(row % requests == request, slot % context < limit)
    row, new = indices(rows)
    seen_new = jnp.logical_and(
        row % requests == new % requests, new // requests <= row // requests
    )
    for head in range(local_width // HEAD_SIZE):
        columns = slice(head * HEAD_SIZE, (head + 1) * HEAD_SIZE)
        query = []
        for one in range(head * group, (head + 1) * group):
            part = slice(one * HEAD_SIZE, (one + 1) * HEAD_SIZE)
            total = returned_ref[0, :, part].astype(F32)
            for z in range(1, Z):
                total += returned_ref[z, :, part].astype(F32)
            query.append(total)
        query = row_scaling(jnp.concatenate(query, axis=0), gain_ref[...])
        query = query * cosine + pltpu.roll(query, HEAD_SIZE // 2, axis=1) * sine
        query = query.astype(BF16)
        transposed = (((1,), (1,)), ((), ()))
        old = lax.dot_general(
            query, keys_ref[:, columns], transposed, preferred_element_type=F32
        ) * scale
        new = lax.dot_general(
            query, new_keys_ref[:, columns], transposed, preferred_element_type=F32
        ) * scale
        old = jnp.where(seen, old, -jnp.inf)
        new = jnp.where(seen_new, new, -jnp.inf)
        top = jnp.maximum(
            jnp.max(old, axis=-1, keepdims=True), jnp.max(new, axis=-1, keepdims=True)
        )
        old_exp = jnp.exp(old - top)
        new_exp = jnp.exp(new - top)
        total = jnp.sum(old_exp, axis=-1, keepdims=True) + jnp.sum(new_exp, axis=-1, keepdims=True)
        mixed = dot((old_exp / total).astype(BF16), values_ref[:, columns])
        mixed += dot((new_exp / total).astype(BF16), new_values_ref[:, columns])
        mixed = mixed.astype(BF16)
        for one in range(group):
            part = head * group + one
            block = mixed[one * rows : (one + 1) * rows]
            for z in range(Z):
                out_ref[z, :, part * HEAD_SIZE : (part + 1) * HEAD_SIZE] = block


def copy_kernel(source_ref, out_ref):
    out_ref[0] = source_ref[...]


def packed(pool, width):
    sides = width // pool.shape[1]
    run = pool.shape[0] // sides
    return jnp.concatenate([pool[i * run : (i + 1) * run] for i in range(sides)], axis=1)


def unpack_kernel(handed_ref, hidden_ref, out_ref, wide_ref):
    wide_ref[...] = hidden_ref[...].astype(F32)
    tokens, sections, width = out_ref.shape[1:]
    sides = handed_ref.shape[1] // (sections * width)
    run = tokens // sides
    for i in range(sides):
        for section in range(sections):
            start = (i * sections + section) * width
            out_ref[0, i * run : (i + 1) * run, section, :] = handed_ref[:, start : start + width]


def shards(
    span_hidden,
    attn_gain,
    kv_weight,
    q_gain,
    key_norm_gain,
    q_weight,
    o_weight,
    decode_hidden,
    cache,
    cache_len,
    block_owner,
    block_slot,
):
    y_index = lax.axis_index("y")
    seq_index = lax.axis_index("z") * Y + y_index
    prefill_side = lax.axis_index("role") == 0
    span_rows = span_hidden.shape[1]
    local_width = kv_weight.shape[2]
    steps, requests, width = decode_hidden.shape
    rows = steps * requests
    depth, local_query = q_weight.shape
    out_depth, out_width = o_weight.shape
    seq_count, block_count = block_owner.shape
    buffer_tokens = seq_count * CAPACITY * BLOCK_TOKENS
    chunk = width // Z
    context = cache.shape[1]
    slots = requests * context
    exchanged = (Z, rows, local_query)

    whole = pl.BlockSpec(memory_space=pltpu.VMEM)
    unwritten = pl.BlockSpec(memory_space=pl.ANY)
    section = jax.ShapeDtypeStruct((span_rows, 2, local_width), BF16)
    buffer = jax.ShapeDtypeStruct((seq_count, CAPACITY * BLOCK_TOKENS, 2 * local_width), BF16)

    def rank_table():
        block_number = jnp.arange(block_count, dtype=jnp.int32)
        same_owner = block_owner[:, :, None] == block_owner[:, None, :]
        earlier = block_number[None, None, :] < block_number[None, :, None]
        return jnp.sum(jnp.logical_and(same_owner, earlier).astype(jnp.int32), axis=2)

    pool_rows = span_rows * 2 * local_width // out_depth
    handed_over = jax.ShapeDtypeStruct((Y * out_width + pool_rows, out_depth), BF16)

    def one_hot(blocks):
        token = lax.broadcasted_iota(jnp.int32, (block_count, BLOCK_TOKENS), 1)
        at = (blocks[:, None] * BLOCK_TOKENS + token).reshape(1, span_rows)
        place = lax.broadcasted_iota(jnp.int32, (buffer_tokens, span_rows), 0)
        return (place == at).astype(BF16)

    def prefill(*_):
        normed = row_scaling(span_hidden[0].astype(F32), attn_gain).astype(BF16)
        projected = jnp.einsum("td,dcw->ctw", normed, kv_weight, preferred_element_type=F32)
        cosine, sine = rotary_tables(seq_index * span_rows + jnp.arange(span_rows, dtype=jnp.int32))
        keys = head_norm_rotary(projected[0], key_norm_gain, cosine, sine)
        span_kv = jnp.concatenate([keys, projected[1]], axis=1).astype(BF16)
        own_owner = lax.dynamic_index_in_dim(block_owner, seq_index, 0, keepdims=False)
        own_rank = lax.dynamic_index_in_dim(rank_table(), seq_index, 0, keepdims=False)
        payload = dot(one_hot(own_owner * CAPACITY + own_rank), span_kv).astype(BF16)
        return (
            jnp.zeros((Z * rows, chunk), BF16),
            jnp.zeros((rows, HEAD_SIZE), F32),
            jnp.zeros((rows, HEAD_SIZE), F32),
            jnp.zeros((rows, local_width), BF16),
            jnp.zeros((rows, local_width), BF16),
            jnp.zeros((slots, local_width), BF16),
            jnp.zeros((slots, local_width), BF16),
            span_kv.reshape(section.shape),
            payload.reshape(buffer.shape),
        )

    def route(payload, *_):
        turned = o_weight.T
        handed = jnp.zeros(handed_over.shape, BF16)
        for shift in range(Y):
            part = turned
            if shift > 0:
                part = lax.ppermute(turned, "y", [(i, (i - shift) % Y) for i in range(Y)])
            handed = lax.dynamic_update_slice(
                handed, part, (lax.rem(y_index + shift, Y) * out_width, 0)
            )
        arrived = lax.all_to_all(payload, SEQ, split_axis=0, concat_axis=0, tiled=True)
        block_number = jnp.arange(block_count, dtype=jnp.int32)
        came_as = jnp.arange(seq_count, dtype=jnp.int32)[:, None] * CAPACITY + rank_table()
        target = jnp.where(block_owner == seq_index, block_slot, -1)
        source = jnp.sum(
            jnp.where(target[None] == block_number[:, None, None], came_as[None], 0), axis=(1, 2)
        )
        pool = lax.dot_general(
            one_hot(source),
            arrived.reshape(buffer_tokens, 2 * local_width),
            (((0,), (0,)), ((), ())),
            preferred_element_type=F32,
        ).astype(BF16)
        handed = lax.dynamic_update_slice(handed, packed(pool, out_depth), (Y * out_width, 0))
        return handed, jnp.zeros(exchanged, BF16)

    arrived_weights = [None] * (Y - 1)
    for shift in (2, 3, 1):
        pairs = [(i, Y + (i - shift) % Y) for i in range(Y)] + [(Y + i, i) for i in range(Y)]
        arrived_weights[shift - 1] = lax.ppermute(q_weight, ("role", "y"), pairs)

    def project(*_):
        spread, normed, span_kv, payload = pl.pallas_call(
            norm_kernel,
            out_shape=(
                jax.ShapeDtypeStruct((Z, rows, chunk), BF16),
                jax.ShapeDtypeStruct((rows, width), BF16),
                section,
                buffer,
            ),
            in_specs=[
                pl.BlockSpec(memory_space=pltpu.SMEM),
                whole,
                whole,
            ],
            out_specs=[whole] * 2 + [unwritten] * 2,
            compiler_params=pltpu.CompilerParams(vmem_limit_bytes=VMEM_LIMIT),
        )(y_index.astype(jnp.int32).reshape(1), decode_hidden, attn_gain.reshape(1, width))
        spread = lax.all_to_all(spread, "z", split_axis=0, concat_axis=0, tiled=True)
        position = (
            cache_len[None, :] + jnp.arange(steps, dtype=jnp.int32)[:, None]
        ).reshape(rows)
        cosine, sine = rotary_tables(position)
        fresh = jnp.einsum("rd,dcw->crw", normed, kv_weight, preferred_element_type=F32)
        new_keys = head_norm_rotary(fresh[0], key_norm_gain, cosine, sine).astype(BF16)
        new_values = fresh[1].astype(BF16)
        cosine = jnp.concatenate([cosine, cosine], axis=1)
        sine = jnp.concatenate([-sine, sine], axis=1)
        spread = spread.reshape(Z * rows, chunk)
        keys = cache[:, :, 0].reshape(slots, local_width)
        values = cache[:, :, 1].reshape(slots, local_width)
        return spread, cosine, sine, new_keys, new_values, keys, values, span_kv, payload

    spread, *beside, span_kv, payload = lax.cond(prefill_side, prefill, project)

    def attend(payload, spread, cosine, sine, new_keys, new_values, keys, values, *weights):
        partial = pl.pallas_call(
            query_kernel,
            in_specs=[whole] * 5,
            out_specs=whole,
            out_shape=jax.ShapeDtypeStruct((Z * rows, local_query), BF16),
            compiler_params=pltpu.CompilerParams(vmem_limit_bytes=VMEM_LIMIT),
        )(spread, q_weight, *weights)
        returned = lax.all_to_all(
            partial.reshape(exchanged), "z", split_axis=0, concat_axis=0, tiled=True
        )
        attended, handed = pl.pallas_call(
            attention_kernel,
            out_shape=(
                jax.ShapeDtypeStruct(exchanged, BF16),
                handed_over,
            ),
            in_specs=[pl.BlockSpec(memory_space=pltpu.SMEM)] + [whole] * 8,
            out_specs=[whole, unwritten],
            compiler_params=pltpu.CompilerParams(vmem_limit_bytes=VMEM_LIMIT),
        )(
            cache_len,
            returned,
            q_gain.reshape(1, HEAD_SIZE),
            cosine,
            sine,
            keys,
            values,
            new_keys,
            new_values,
        )
        return handed, attended

    handed, attended = lax.cond(
        prefill_side, route, attend,
        payload, spread, *beside, *arrived_weights,
    )
    handed = lax.ppermute(handed, "role", [(0, 1)])

    def gather(attended):
        return lax.all_to_all(attended, "z", split_axis=0, concat_axis=0, tiled=True)

    attended = lax.cond(prefill_side, lambda attended: attended, gather, attended)

    limited = pltpu.CompilerParams(vmem_limit_bytes=VMEM_LIMIT)
    placed = jax.ShapeDtypeStruct((1,) + section.shape, BF16)

    def finish(attended, span_kv, handed):
        partial = lax.dot_general(
            attended.reshape(Z * rows, local_query),
            handed,
            (((1,), (1,)), ((), ())),
            preferred_element_type=F32,
        )[:, : Y * out_width].astype(BF16)
        back = lax.all_to_all(
            partial.reshape(Z, rows, chunk), "z", split_axis=0, concat_axis=0, tiled=True
        )
        tp_count = lax.axis_size("tp")
        delta = back.astype(F32)
        for shift in range(1, tp_count):
            pairs = [(i, (i + shift) % tp_count) for i in range(tp_count)]
            delta = delta + lax.ppermute(back, "tp", pairs).astype(F32)
        delta = delta.transpose(1, 0, 2).reshape(steps, requests, width)
        pool, hidden = pl.pallas_call(
            unpack_kernel,
            grid=(1,),
            in_specs=[
                pl.BlockSpec((pool_rows, out_depth), lambda i: (Y * out_width // pool_rows, 0)),
                pl.BlockSpec((steps, requests, width), lambda i: (0, 0, 0)),
            ],
            out_specs=[
                pl.BlockSpec(placed.shape, lambda i: (0, 0, 0, 0)),
                pl.BlockSpec((steps, requests, width), lambda i: (0, 0, 0)),
            ],
            out_shape=(placed, jax.ShapeDtypeStruct((steps, requests, width), F32)),
            compiler_params=limited,
        )(handed, decode_hidden)
        return pool, (hidden + delta).astype(BF16)[None]

    def idle_finish(attended, span_kv, handed):
        span = pl.pallas_call(
            copy_kernel, in_specs=[whole], out_specs=whole, out_shape=placed, compiler_params=limited
        )(span_kv)
        return span, jnp.zeros((1, steps, requests, width), BF16)

    return lax.cond(prefill_side, idle_finish, finish, attended, span_kv, handed)


def solution(mesh):
    shape = mesh.devices.shape
    fine = Mesh(mesh.devices.reshape(shape[0], Z, Y, shape[2]), ("role", "z", "y", "tp"))
    placed = (
        P("role", SEQ, None),
        P(),
        P(None, None, "tp"),
        P(),
        P(),
        P(SEQ, "tp"),
        P("tp", SEQ),
        P(None, SEQ, None),
        P(SEQ, None, None, "tp"),
        P(SEQ),
        P(),
        P(),
    )
    return jax.shard_map(
        shards,
        mesh=fine,
        in_specs=placed,
        out_specs=(P("role", SEQ, None, "tp"), P("role", None, SEQ, None)),
        check_vma=False,
    )
```

```python
import math

import jax
import jax.numpy as jnp
from jax import lax
from jax.experimental import pallas as pl
from jax.experimental.pallas import tpu as pltpu
from jax.sharding import Mesh, PartitionSpec as P

QUERY_HEADS = 64
KEY_VALUE_HEADS = 8
HEAD_SIZE = 128
EPSILON = 1e-06
THETA_BASE = 1000000.0

Z, Y = 8, 4
SEQ = ("z", "y")
BLOCK_TOKENS = 8
CAPACITY = 2
VMEM_LIMIT = 8 * 2**20
F32, BF16 = jnp.float32, jnp.bfloat16


def row_scaling(values, weights):
    return values * lax.rsqrt(jnp.mean(values * values, axis=-1, keepdims=True) + EPSILON) * weights


def rotary_tables(token_position):
    half_dim = HEAD_SIZE // 2
    frequency = jnp.exp(
        jnp.arange(half_dim, dtype=F32) * (-2.0 * math.log(THETA_BASE) / HEAD_SIZE)
    )
    angles = token_position.astype(F32)[:, None] * frequency
    return jnp.cos(angles), jnp.sin(angles)


def apply_rotary(values, cosine, sine):
    half_dim = HEAD_SIZE // 2
    first_half = values[..., :half_dim]
    second_half = values[..., half_dim:]
    return jnp.concatenate(
        [first_half * cosine - second_half * sine, second_half * cosine + first_half * sine],
        axis=-1,
    )


def head_norm_rotary(values, gain, cosine, sine):
    rows, width = values.shape
    heads = values.reshape(rows, width // HEAD_SIZE, HEAD_SIZE)
    turned = apply_rotary(row_scaling(heads, gain), cosine[:, None, :], sine[:, None, :])
    return turned.reshape(rows, width)


def dot(a, b):
    return jnp.dot(a, b, preferred_element_type=F32)


def norm_kernel(y_ref, hidden_ref, gain_ref, spread_ref, normed_ref, *unused):
    hidden = jnp.concatenate(
        [hidden_ref[step].astype(F32) for step in range(hidden_ref.shape[0])], axis=0
    )
    normed = row_scaling(hidden, gain_ref[...])
    normed_ref[...] = normed.astype(BF16)
    chunk = spread_ref.shape[2]
    shift = lax.rem(Y - y_ref[0], Y) * (chunk // Y)
    for z in range(Z):
        block = normed[:, z * chunk : (z + 1) * chunk]
        spread_ref[z] = pltpu.roll(block, shift, axis=1).astype(BF16)


def query_kernel(rows_ref, own_ref, first_ref, second_ref, third_ref, out_ref):
    tile = 512
    for start in range(0, out_ref.shape[1], tile):
        columns = slice(start, start + tile)
        weight = jnp.concatenate(
            [ref[:, columns] for ref in (own_ref, first_ref, second_ref, third_ref)], axis=0
        )
        out_ref[:, columns] = dot(rows_ref[...], weight).astype(BF16)


def attention_kernel(
    length_ref,
    returned_ref,
    gain_ref,
    cosine_ref,
    sine_ref,
    keys_ref,
    values_ref,
    new_keys_ref,
    new_values_ref,
    out_ref,
    *unused,
):
    rows = returned_ref.shape[1]
    requests = rows // 4
    slots, local_width = keys_ref.shape
    context = slots // requests
    group = returned_ref.shape[2] // local_width
    scale = HEAD_SIZE ** (-0.5)
    cosine = jnp.concatenate([cosine_ref[...]] * group, axis=0)
    sine = jnp.concatenate([sine_ref[...]] * group, axis=0)

    def indices(columns):
        row = lax.broadcasted_iota(jnp.int32, (group * rows, columns), 0) % rows
        return row, lax.broadcasted_iota(jnp.int32, (group * rows, columns), 1)

    row, slot = indices(slots)
    request = slot // context
    limit = jnp.full_like(slot, length_ref[0])
    for one in range(1, requests):
        limit = jnp.where(request == one, length_ref[one], limit)
    seen = jnp.logical_and(row % requests == request, slot % context < limit)
    row, new = indices(rows)
    seen_new = jnp.logical_and(
        row % requests == new % requests, new // requests <= row // requests
    )
    for head in range(local_width // HEAD_SIZE):
        columns = slice(head * HEAD_SIZE, (head + 1) * HEAD_SIZE)
        query = []
        for one in range(head * group, (head + 1) * group):
            part = slice(one * HEAD_SIZE, (one + 1) * HEAD_SIZE)
            total = returned_ref[0, :, part].astype(F32)
            for z in range(1, Z):
                total += returned_ref[z, :, part].astype(F32)
            query.append(total)
        query = row_scaling(jnp.concatenate(query, axis=0), gain_ref[...])
        query = query * cosine + pltpu.roll(query, HEAD_SIZE // 2, axis=1) * sine
        query = query.astype(BF16)
        transposed = (((1,), (1,)), ((), ()))
        old = lax.dot_general(
            query, keys_ref[:, columns], transposed, preferred_element_type=F32
        ) * scale
        new = lax.dot_general(
            query, new_keys_ref[:, columns], transposed, preferred_element_type=F32
        ) * scale
        old = jnp.where(seen, old, -jnp.inf)
        new = jnp.where(seen_new, new, -jnp.inf)
        top = jnp.maximum(
            jnp.max(old, axis=-1, keepdims=True), jnp.max(new, axis=-1, keepdims=True)
        )
        old_exp = jnp.exp(old - top)
        new_exp = jnp.exp(new - top)
        total = jnp.sum(old_exp, axis=-1, keepdims=True) + jnp.sum(new_exp, axis=-1, keepdims=True)
        mixed = dot((old_exp / total).astype(BF16), values_ref[:, columns])
        mixed += dot((new_exp / total).astype(BF16), new_values_ref[:, columns])
        mixed = mixed.astype(BF16)
        for one in range(group):
            part = head * group + one
            block = mixed[one * rows : (one + 1) * rows]
            for z in range(Z):
                out_ref[z, :, part * HEAD_SIZE : (part + 1) * HEAD_SIZE] = block


def copy_kernel(source_ref, out_ref):
    out_ref[0] = source_ref[...]


def packed(pool, width):
    sides = width // pool.shape[1]
    run = pool.shape[0] // sides
    return jnp.concatenate([pool[i * run : (i + 1) * run] for i in range(sides)], axis=1)


def unpack_kernel(handed_ref, hidden_ref, out_ref, wide_ref):
    wide_ref[...] = hidden_ref[...].astype(F32)
    tokens, sections, width = out_ref.shape[1:]
    sides = handed_ref.shape[1] // (sections * width)
    run = tokens // sides
    for i in range(sides):
        parts = []
        for section in range(sections):
            start = (i * sections + section) * width
            parts.append(handed_ref[:, start : start + width].astype(F32)[:, None, :])
        run_kv = jnp.concatenate(parts, axis=1).astype(out_ref.dtype)
        out_ref[0, i * run : (i + 1) * run] = run_kv


def shards(
    span_hidden,
    attn_gain,
    kv_weight,
    q_gain,
    key_norm_gain,
    q_weight,
    o_weight,
    decode_hidden,
    cache,
    cache_len,
    block_owner,
    block_slot,
):
    y_index = lax.axis_index("y")
    seq_index = lax.axis_index("z") * Y + y_index
    prefill_side = lax.axis_index("role") == 0
    span_rows = span_hidden.shape[1]
    local_width = kv_weight.shape[2]
    steps, requests, width = decode_hidden.shape
    rows = steps * requests
    depth, local_query = q_weight.shape
    out_depth, out_width = o_weight.shape
    seq_count, block_count = block_owner.shape
    buffer_tokens = seq_count * CAPACITY * BLOCK_TOKENS
    chunk = width // Z
    context = cache.shape[1]
    slots = requests * context
    exchanged = (Z, rows, local_query)

    whole = pl.BlockSpec(memory_space=pltpu.VMEM)
    unwritten = pl.BlockSpec(memory_space=pl.ANY)
    section = jax.ShapeDtypeStruct((span_rows, 2, local_width), BF16)
    buffer = jax.ShapeDtypeStruct((seq_count, CAPACITY * BLOCK_TOKENS, 2 * local_width), BF16)

    def rank_table():
        block_number = jnp.arange(block_count, dtype=jnp.int32)
        same_owner = block_owner[:, :, None] == block_owner[:, None, :]
        earlier = block_number[None, None, :] < block_number[None, :, None]
        return jnp.sum(jnp.logical_and(same_owner, earlier).astype(jnp.int32), axis=2)

    pool_rows = span_rows * 2 * local_width // out_depth
    handed_over = jax.ShapeDtypeStruct((Y * out_width + pool_rows, out_depth), BF16)

    def one_hot(blocks):
        token = lax.broadcasted_iota(jnp.int32, (block_count, BLOCK_TOKENS), 1)
        at = (blocks[:, None] * BLOCK_TOKENS + token).reshape(1, span_rows)
        place = lax.broadcasted_iota(jnp.int32, (buffer_tokens, span_rows), 0)
        return (place == at).astype(BF16)

    def prefill(*_):
        normed = row_scaling(span_hidden[0].astype(F32), attn_gain).astype(BF16)
        projected = jnp.einsum("td,dcw->ctw", normed, kv_weight, preferred_element_type=F32)
        cosine, sine = rotary_tables(seq_index * span_rows + jnp.arange(span_rows, dtype=jnp.int32))
        keys = head_norm_rotary(projected[0], key_norm_gain, cosine, sine)
        span_kv = jnp.concatenate([keys, projected[1]], axis=1).astype(BF16)
        own_owner = lax.dynamic_index_in_dim(block_owner, seq_index, 0, keepdims=False)
        own_rank = lax.dynamic_index_in_dim(rank_table(), seq_index, 0, keepdims=False)
        payload = dot(one_hot(own_owner * CAPACITY + own_rank), span_kv).astype(BF16)
        return (
            jnp.zeros((Z * rows, chunk), BF16),
            jnp.zeros((rows, HEAD_SIZE), F32),
            jnp.zeros((rows, HEAD_SIZE), F32),
            jnp.zeros((rows, local_width), BF16),
            jnp.zeros((rows, local_width), BF16),
            jnp.zeros((slots, local_width), BF16),
            jnp.zeros((slots, local_width), BF16),
            span_kv.reshape(section.shape),
            payload.reshape(buffer.shape),
        )

    def route(payload, *_):
        turned = o_weight.T
        handed = jnp.zeros(handed_over.shape, BF16)
        for shift in range(Y):
            part = turned
            if shift > 0:
                part = lax.ppermute(turned, "y", [(i, (i - shift) % Y) for i in range(Y)])
            handed = lax.dynamic_update_slice(
                handed, part, (lax.rem(y_index + shift, Y) * out_width, 0)
            )
        arrived = lax.all_to_all(payload, SEQ, split_axis=0, concat_axis=0, tiled=True)
        block_number = jnp.arange(block_count, dtype=jnp.int32)
        came_as = jnp.arange(seq_count, dtype=jnp.int32)[:, None] * CAPACITY + rank_table()
        target = jnp.where(block_owner == seq_index, block_slot, -1)
        source = jnp.sum(
            jnp.where(target[None] == block_number[:, None, None], came_as[None], 0), axis=(1, 2)
        )
        pool = lax.dot_general(
            one_hot(source),
            arrived.reshape(buffer_tokens, 2 * local_width),
            (((0,), (0,)), ((), ())),
            preferred_element_type=F32,
        ).astype(BF16)
        handed = lax.dynamic_update_slice(handed, packed(pool, out_depth), (Y * out_width, 0))
        return handed, jnp.zeros(exchanged, BF16)

    arrived_weights = [None] * (Y - 1)
    for shift in (2, 3, 1):
        pairs = [(i, Y + (i - shift) % Y) for i in range(Y)] + [(Y + i, i) for i in range(Y)]
        arrived_weights[shift - 1] = lax.ppermute(q_weight, ("role", "y"), pairs)

    def project(*_):
        spread, normed, span_kv, payload = pl.pallas_call(
            norm_kernel,
            out_shape=(
                jax.ShapeDtypeStruct((Z, rows, chunk), BF16),
                jax.ShapeDtypeStruct((rows, width), BF16),
                section,
                buffer,
            ),
            in_specs=[
                pl.BlockSpec(memory_space=pltpu.SMEM),
                whole,
                whole,
            ],
            out_specs=[whole] * 2 + [unwritten] * 2,
            compiler_params=pltpu.CompilerParams(vmem_limit_bytes=VMEM_LIMIT),
        )(y_index.astype(jnp.int32).reshape(1), decode_hidden, attn_gain.reshape(1, width))
        spread = lax.all_to_all(spread, "z", split_axis=0, concat_axis=0, tiled=True)
        position = (
            cache_len[None, :] + jnp.arange(steps, dtype=jnp.int32)[:, None]
        ).reshape(rows)
        cosine, sine = rotary_tables(position)
        fresh = jnp.einsum("rd,dcw->crw", normed, kv_weight, preferred_element_type=F32)
        new_keys = head_norm_rotary(fresh[0], key_norm_gain, cosine, sine).astype(BF16)
        new_values = fresh[1].astype(BF16)
        cosine = jnp.concatenate([cosine, cosine], axis=1)
        sine = jnp.concatenate([-sine, sine], axis=1)
        spread = spread.reshape(Z * rows, chunk)
        keys = cache[:, :, 0].reshape(slots, local_width)
        values = cache[:, :, 1].reshape(slots, local_width)
        return spread, cosine, sine, new_keys, new_values, keys, values, span_kv, payload

    spread, *beside, span_kv, payload = lax.cond(prefill_side, prefill, project)

    def attend(payload, spread, cosine, sine, new_keys, new_values, keys, values, *weights):
        partial = pl.pallas_call(
            query_kernel,
            in_specs=[whole] * 5,
            out_specs=whole,
            out_shape=jax.ShapeDtypeStruct((Z * rows, local_query), BF16),
            compiler_params=pltpu.CompilerParams(vmem_limit_bytes=VMEM_LIMIT),
        )(spread, q_weight, *weights)
        returned = lax.all_to_all(
            partial.reshape(exchanged), "z", split_axis=0, concat_axis=0, tiled=True
        )
        attended, handed = pl.pallas_call(
            attention_kernel,
            out_shape=(
                jax.ShapeDtypeStruct(exchanged, BF16),
                handed_over,
            ),
            in_specs=[pl.BlockSpec(memory_space=pltpu.SMEM)] + [whole] * 8,
            out_specs=[whole, unwritten],
            compiler_params=pltpu.CompilerParams(vmem_limit_bytes=VMEM_LIMIT),
        )(
            cache_len,
            returned,
            q_gain.reshape(1, HEAD_SIZE),
            cosine,
            sine,
            keys,
            values,
            new_keys,
            new_values,
        )
        return handed, attended

    handed, attended = lax.cond(
        prefill_side, route, attend,
        payload, spread, *beside, *arrived_weights,
    )
    handed = lax.ppermute(handed, "role", [(0, 1)])

    def gather(attended):
        return lax.all_to_all(attended, "z", split_axis=0, concat_axis=0, tiled=True)

    attended = lax.cond(prefill_side, lambda attended: attended, gather, attended)

    limited = pltpu.CompilerParams(vmem_limit_bytes=VMEM_LIMIT)
    placed = jax.ShapeDtypeStruct((1,) + section.shape, BF16)

    def finish(attended, span_kv, handed):
        partial = lax.dot_general(
            attended.reshape(Z * rows, local_query),
            handed,
            (((1,), (1,)), ((), ())),
            preferred_element_type=F32,
        )[:, : Y * out_width].astype(BF16)
        back = lax.all_to_all(
            partial.reshape(Z, rows, chunk), "z", split_axis=0, concat_axis=0, tiled=True
        )
        tp_count = lax.axis_size("tp")
        delta = back.astype(F32)
        for shift in sorted(range(1, tp_count), key=lambda shift: -min(shift, tp_count - shift)):
            pairs = [(i, (i + shift) % tp_count) for i in range(tp_count)]
            delta = delta + lax.ppermute(back, "tp", pairs).astype(F32)
        delta = delta.transpose(1, 0, 2).reshape(steps, requests, width)
        pool, hidden = pl.pallas_call(
            unpack_kernel,
            grid=(1,),
            in_specs=[
                pl.BlockSpec((pool_rows, out_depth), lambda i: (Y * out_width // pool_rows, 0)),
                pl.BlockSpec((steps, requests, width), lambda i: (0, 0, 0)),
            ],
            out_specs=[
                pl.BlockSpec(placed.shape, lambda i: (0, 0, 0, 0)),
                pl.BlockSpec((steps, requests, width), lambda i: (0, 0, 0)),
            ],
            out_shape=(placed, jax.ShapeDtypeStruct((steps, requests, width), F32)),
            compiler_params=limited,
        )(handed, decode_hidden)
        return pool, (hidden + delta).astype(BF16)[None]

    def idle_finish(attended, span_kv, handed):
        span = pl.pallas_call(
            copy_kernel, in_specs=[whole], out_specs=whole, out_shape=placed, compiler_params=limited
        )(span_kv)
        return span, jnp.zeros((1, steps, requests, width), BF16)

    return lax.cond(prefill_side, idle_finish, finish, attended, span_kv, handed)


def solution(mesh):
    shape = mesh.devices.shape
    fine = Mesh(mesh.devices.reshape(shape[0], Z, Y, shape[2]), ("role", "z", "y", "tp"))
    placed = (
        P("role", SEQ, None),
        P(),
        P(None, None, "tp"),
        P(),
        P(),
        P(SEQ, "tp"),
        P("tp", SEQ),
        P(None, SEQ, None),
        P(SEQ, None, None, "tp"),
        P(SEQ),
        P(),
        P(),
    )
    return jax.shard_map(
        shards,
        mesh=fine,
        in_specs=placed,
        out_specs=(P("role", SEQ, None, "tp"), P("role", None, SEQ, None)),
        check_vma=False,
    )
```

```python
import math

import jax
import jax.numpy as jnp
from jax import lax
from jax.experimental import pallas as pl
from jax.experimental.pallas import tpu as pltpu
from jax.sharding import Mesh, PartitionSpec as P

QUERY_HEADS = 64
KEY_VALUE_HEADS = 8
HEAD_SIZE = 128
EPSILON = 1e-06
THETA_BASE = 1000000.0

Z, Y = 8, 4
SEQ = ("z", "y")
BLOCK_TOKENS = 8
CAPACITY = 2
VMEM_LIMIT = 8 * 2**20
F32, BF16 = jnp.float32, jnp.bfloat16


def row_scaling(values, weights):
    return values * lax.rsqrt(jnp.mean(values * values, axis=-1, keepdims=True) + EPSILON) * weights


def rotary_tables(token_position):
    half_dim = HEAD_SIZE // 2
    frequency = jnp.exp(
        jnp.arange(half_dim, dtype=F32) * (-2.0 * math.log(THETA_BASE) / HEAD_SIZE)
    )
    angles = token_position.astype(F32)[:, None] * frequency
    return jnp.cos(angles), jnp.sin(angles)


def apply_rotary(values, cosine, sine):
    half_dim = HEAD_SIZE // 2
    first_half = values[..., :half_dim]
    second_half = values[..., half_dim:]
    return jnp.concatenate(
        [first_half * cosine - second_half * sine, second_half * cosine + first_half * sine],
        axis=-1,
    )


def head_norm_rotary(values, gain, cosine, sine):
    rows, width = values.shape
    heads = values.reshape(rows, width // HEAD_SIZE, HEAD_SIZE)
    turned = apply_rotary(row_scaling(heads, gain), cosine[:, None, :], sine[:, None, :])
    return turned.reshape(rows, width)


def dot(a, b):
    return jnp.dot(a, b, preferred_element_type=F32)


def norm_kernel(y_ref, hidden_ref, gain_ref, spread_ref, normed_ref, *unused):
    hidden = jnp.concatenate(
        [hidden_ref[step].astype(F32) for step in range(hidden_ref.shape[0])], axis=0
    )
    normed = row_scaling(hidden, gain_ref[...])
    normed_ref[...] = normed.astype(BF16)
    chunk = spread_ref.shape[2]
    shift = lax.rem(Y - y_ref[0], Y) * (chunk // Y)
    for z in range(Z):
        block = normed[:, z * chunk : (z + 1) * chunk]
        spread_ref[z] = pltpu.roll(block, shift, axis=1).astype(BF16)


def query_kernel(
    rows_ref, own_ref, first_ref, second_ref, third_ref, out_ref, last_ref, total_ref, semaphore
):
    copy = pltpu.make_async_copy(third_ref, last_ref, semaphore)
    copy.start()
    tile = 512
    depth = 3 * own_ref.shape[0]
    tiles = [slice(start, start + tile) for start in range(0, out_ref.shape[1], tile)]
    for columns in tiles:
        weight = jnp.concatenate(
            [ref[:, columns] for ref in (own_ref, first_ref, second_ref)], axis=0
        )
        total_ref[:, columns] = dot(rows_ref[:, :depth], weight)
    copy.wait()
    for columns in tiles:
        last = dot(rows_ref[:, depth:], last_ref[:, columns])
        out_ref[:, columns] = (total_ref[:, columns] + last).astype(BF16)


def attention_kernel(
    length_ref,
    returned_ref,
    gain_ref,
    cosine_ref,
    sine_ref,
    keys_ref,
    values_ref,
    new_keys_ref,
    new_values_ref,
    out_ref,
    *unused,
):
    rows = returned_ref.shape[1]
    requests = rows // 4
    slots, local_width = keys_ref.shape
    context = slots // requests
    group = returned_ref.shape[2] // local_width
    scale = HEAD_SIZE ** (-0.5)
    cosine = jnp.concatenate([cosine_ref[...]] * group, axis=0)
    sine = jnp.concatenate([sine_ref[...]] * group, axis=0)

    def indices(columns):
        row = lax.broadcasted_iota(jnp.int32, (group * rows, columns), 0) % rows
        return row, lax.broadcasted_iota(jnp.int32, (group * rows, columns), 1)

    row, slot = indices(slots)
    request = slot // context
    limit = jnp.full_like(slot, length_ref[0])
    for one in range(1, requests):
        limit = jnp.where(request == one, length_ref[one], limit)
    seen = jnp.logical_and(row % requests == request, slot % context < limit)
    row, new = indices(rows)
    seen_new = jnp.logical_and(
        row % requests == new % requests, new // requests <= row // requests
    )
    for head in range(local_width // HEAD_SIZE):
        columns = slice(head * HEAD_SIZE, (head + 1) * HEAD_SIZE)
        query = []
        for one in range(head * group, (head + 1) * group):
            part = slice(one * HEAD_SIZE, (one + 1) * HEAD_SIZE)
            total = returned_ref[0, :, part].astype(F32)
            for z in range(1, Z):
                total += returned_ref[z, :, part].astype(F32)
            query.append(total)
        query = row_scaling(jnp.concatenate(query, axis=0), gain_ref[...])
        query = query * cosine + pltpu.roll(query, HEAD_SIZE // 2, axis=1) * sine
        query = query.astype(BF16)
        transposed = (((1,), (1,)), ((), ()))
        old = lax.dot_general(
            query, keys_ref[:, columns], transposed, preferred_element_type=F32
        ) * scale
        new = lax.dot_general(
            query, new_keys_ref[:, columns], transposed, preferred_element_type=F32
        ) * scale
        old = jnp.where(seen, old, -jnp.inf)
        new = jnp.where(seen_new, new, -jnp.inf)
        top = jnp.maximum(
            jnp.max(old, axis=-1, keepdims=True), jnp.max(new, axis=-1, keepdims=True)
        )
        old_exp = jnp.exp(old - top)
        new_exp = jnp.exp(new - top)
        total = jnp.sum(old_exp, axis=-1, keepdims=True) + jnp.sum(new_exp, axis=-1, keepdims=True)
        mixed = dot((old_exp / total).astype(BF16), values_ref[:, columns])
        mixed += dot((new_exp / total).astype(BF16), new_values_ref[:, columns])
        mixed = mixed.astype(BF16)
        for one in range(group):
            part = head * group + one
            block = mixed[one * rows : (one + 1) * rows]
            for z in range(Z):
                out_ref[z, :, part * HEAD_SIZE : (part + 1) * HEAD_SIZE] = block


def copy_kernel(source_ref, out_ref):
    out_ref[0] = source_ref[...]


def packed(pool, width):
    sides = width // pool.shape[1]
    run = pool.shape[0] // sides
    return jnp.concatenate([pool[i * run : (i + 1) * run] for i in range(sides)], axis=1)


def unpack_kernel(handed_ref, hidden_ref, out_ref, wide_ref):
    wide_ref[...] = hidden_ref[...].astype(F32)
    tokens, sections, width = out_ref.shape[1:]
    sides = handed_ref.shape[1] // (sections * width)
    run = tokens // sides
    for i in range(sides):
        parts = []
        for section in range(sections):
            start = (i * sections + section) * width
            parts.append(handed_ref[:, start : start + width].astype(F32)[:, None, :])
        run_kv = jnp.concatenate(parts, axis=1).astype(out_ref.dtype)
        out_ref[0, i * run : (i + 1) * run] = run_kv


def shards(
    span_hidden,
    attn_gain,
    kv_weight,
    q_gain,
    key_norm_gain,
    q_weight,
    o_weight,
    decode_hidden,
    cache,
    cache_len,
    block_owner,
    block_slot,
):
    y_index = lax.axis_index("y")
    seq_index = lax.axis_index("z") * Y + y_index
    prefill_side = lax.axis_index("role") == 0
    span_rows = span_hidden.shape[1]
    local_width = kv_weight.shape[2]
    steps, requests, width = decode_hidden.shape
    rows = steps * requests
    depth, local_query = q_weight.shape
    out_depth, out_width = o_weight.shape
    seq_count, block_count = block_owner.shape
    buffer_tokens = seq_count * CAPACITY * BLOCK_TOKENS
    chunk = width // Z
    context = cache.shape[1]
    slots = requests * context
    exchanged = (Z, rows, local_query)

    whole = pl.BlockSpec(memory_space=pltpu.VMEM)
    unwritten = anywhere = pl.BlockSpec(memory_space=pl.ANY)
    section = jax.ShapeDtypeStruct((span_rows, 2, local_width), BF16)
    buffer = jax.ShapeDtypeStruct((seq_count, CAPACITY * BLOCK_TOKENS, 2 * local_width), BF16)

    def rank_table():
        block_number = jnp.arange(block_count, dtype=jnp.int32)
        same_owner = block_owner[:, :, None] == block_owner[:, None, :]
        earlier = block_number[None, None, :] < block_number[None, :, None]
        return jnp.sum(jnp.logical_and(same_owner, earlier).astype(jnp.int32), axis=2)

    pool_rows = span_rows * 2 * local_width // out_depth
    handed_over = jax.ShapeDtypeStruct((Y * out_width + pool_rows, out_depth), BF16)

    def one_hot(blocks):
        token = lax.broadcasted_iota(jnp.int32, (block_count, BLOCK_TOKENS), 1)
        at = (blocks[:, None] * BLOCK_TOKENS + token).reshape(1, span_rows)
        place = lax.broadcasted_iota(jnp.int32, (buffer_tokens, span_rows), 0)
        return (place == at).astype(BF16)

    def prefill(*_):
        normed = row_scaling(span_hidden[0].astype(F32), attn_gain).astype(BF16)
        projected = jnp.einsum("td,dcw->ctw", normed, kv_weight, preferred_element_type=F32)
        cosine, sine = rotary_tables(seq_index * span_rows + jnp.arange(span_rows, dtype=jnp.int32))
        keys = head_norm_rotary(projected[0], key_norm_gain, cosine, sine)
        span_kv = jnp.concatenate([keys, projected[1]], axis=1).astype(BF16)
        own_owner = lax.dynamic_index_in_dim(block_owner, seq_index, 0, keepdims=False)
        own_rank = lax.dynamic_index_in_dim(rank_table(), seq_index, 0, keepdims=False)
        payload = dot(one_hot(own_owner * CAPACITY + own_rank), span_kv).astype(BF16)
        return (
            jnp.zeros((Z * rows, chunk), BF16),
            jnp.zeros((rows, HEAD_SIZE), F32),
            jnp.zeros((rows, HEAD_SIZE), F32),
            jnp.zeros((rows, local_width), BF16),
            jnp.zeros((rows, local_width), BF16),
            jnp.zeros((slots, local_width), BF16),
            jnp.zeros((slots, local_width), BF16),
            span_kv.reshape(section.shape),
            payload.reshape(buffer.shape),
        )

    def route(payload, *_):
        turned = o_weight.T
        handed = jnp.zeros(handed_over.shape, BF16)
        for shift in range(Y):
            part = turned
            if shift > 0:
                part = lax.ppermute(turned, "y", [(i, (i - shift) % Y) for i in range(Y)])
            handed = lax.dynamic_update_slice(
                handed, part, (lax.rem(y_index + shift, Y) * out_width, 0)
            )
        arrived = lax.all_to_all(payload, SEQ, split_axis=0, concat_axis=0, tiled=True)
        block_number = jnp.arange(block_count, dtype=jnp.int32)
        came_as = jnp.arange(seq_count, dtype=jnp.int32)[:, None] * CAPACITY + rank_table()
        target = jnp.where(block_owner == seq_index, block_slot, -1)
        source = jnp.sum(
            jnp.where(target[None] == block_number[:, None, None], came_as[None], 0), axis=(1, 2)
        )
        pool = lax.dot_general(
            one_hot(source),
            arrived.reshape(buffer_tokens, 2 * local_width),
            (((0,), (0,)), ((), ())),
            preferred_element_type=F32,
        ).astype(BF16)
        handed = lax.dynamic_update_slice(handed, packed(pool, out_depth), (Y * out_width, 0))
        return handed, jnp.zeros(exchanged, BF16)

    arrived_weights = [None] * (Y - 1)
    for shift in (2, 3, 1):
        pairs = [(i, Y + (i - shift) % Y) for i in range(Y)] + [(Y + i, i) for i in range(Y)]
        arrived_weights[shift - 1] = lax.ppermute(q_weight, ("role", "y"), pairs)

    def project(*_):
        spread, normed, span_kv, payload = pl.pallas_call(
            norm_kernel,
            out_shape=(
                jax.ShapeDtypeStruct((Z, rows, chunk), BF16),
                jax.ShapeDtypeStruct((rows, width), BF16),
                section,
                buffer,
            ),
            in_specs=[
                pl.BlockSpec(memory_space=pltpu.SMEM),
                whole,
                whole,
            ],
            out_specs=[whole] * 2 + [unwritten] * 2,
            compiler_params=pltpu.CompilerParams(vmem_limit_bytes=VMEM_LIMIT),
        )(y_index.astype(jnp.int32).reshape(1), decode_hidden, attn_gain.reshape(1, width))
        spread = lax.all_to_all(spread, "z", split_axis=0, concat_axis=0, tiled=True)
        position = (
            cache_len[None, :] + jnp.arange(steps, dtype=jnp.int32)[:, None]
        ).reshape(rows)
        cosine, sine = rotary_tables(position)
        fresh = jnp.einsum("rd,dcw->crw", normed, kv_weight, preferred_element_type=F32)
        new_keys = head_norm_rotary(fresh[0], key_norm_gain, cosine, sine).astype(BF16)
        new_values = fresh[1].astype(BF16)
        cosine = jnp.concatenate([cosine, cosine], axis=1)
        sine = jnp.concatenate([-sine, sine], axis=1)
        spread = spread.reshape(Z * rows, chunk)
        keys = cache[:, :, 0].reshape(slots, local_width)
        values = cache[:, :, 1].reshape(slots, local_width)
        return spread, cosine, sine, new_keys, new_values, keys, values, span_kv, payload

    spread, *beside, span_kv, payload = lax.cond(prefill_side, prefill, project)

    def attend(payload, spread, cosine, sine, new_keys, new_values, keys, values, *weights):
        partial = pl.pallas_call(
            query_kernel,
            in_specs=[whole] * 4 + [anywhere],
            out_specs=whole,
            out_shape=jax.ShapeDtypeStruct((Z * rows, local_query), BF16),
            scratch_shapes=[
                pltpu.VMEM((depth, local_query), BF16),
                pltpu.VMEM((Z * rows, local_query), F32),
                pltpu.SemaphoreType.DMA,
            ],
            compiler_params=pltpu.CompilerParams(vmem_limit_bytes=VMEM_LIMIT),
        )(spread, q_weight, *weights)
        returned = lax.all_to_all(
            partial.reshape(exchanged), "z", split_axis=0, concat_axis=0, tiled=True
        )
        attended, handed = pl.pallas_call(
            attention_kernel,
            out_shape=(
                jax.ShapeDtypeStruct(exchanged, BF16),
                handed_over,
            ),
            in_specs=[pl.BlockSpec(memory_space=pltpu.SMEM)] + [whole] * 8,
            out_specs=[whole, unwritten],
            compiler_params=pltpu.CompilerParams(vmem_limit_bytes=VMEM_LIMIT),
        )(
            cache_len,
            returned,
            q_gain.reshape(1, HEAD_SIZE),
            cosine,
            sine,
            keys,
            values,
            new_keys,
            new_values,
        )
        return handed, attended

    handed, attended = lax.cond(
        prefill_side, route, attend,
        payload, spread, *beside, *arrived_weights,
    )
    handed = lax.ppermute(handed, "role", [(0, 1)])

    def gather(attended):
        return lax.all_to_all(attended, "z", split_axis=0, concat_axis=0, tiled=True)

    attended = lax.cond(prefill_side, lambda attended: attended, gather, attended)

    limited = pltpu.CompilerParams(vmem_limit_bytes=VMEM_LIMIT)
    placed = jax.ShapeDtypeStruct((1,) + section.shape, BF16)

    def finish(attended, span_kv, handed):
        partial = lax.dot_general(
            attended.reshape(Z * rows, local_query),
            handed,
            (((1,), (1,)), ((), ())),
            preferred_element_type=F32,
        )[:, : Y * out_width].astype(BF16)
        back = lax.all_to_all(
            partial.reshape(Z, rows, chunk), "z", split_axis=0, concat_axis=0, tiled=True
        )
        tp_count = lax.axis_size("tp")
        delta = back.astype(F32)
        for shift in sorted(range(1, tp_count), key=lambda shift: -min(shift, tp_count - shift)):
            pairs = [(i, (i + shift) % tp_count) for i in range(tp_count)]
            delta = delta + lax.ppermute(back, "tp", pairs).astype(F32)
        delta = delta.transpose(1, 0, 2).reshape(steps, requests, width)
        pool, hidden = pl.pallas_call(
            unpack_kernel,
            grid=(1,),
            in_specs=[
                pl.BlockSpec((pool_rows, out_depth), lambda i: (Y * out_width // pool_rows, 0)),
                pl.BlockSpec((steps, requests, width), lambda i: (0, 0, 0)),
            ],
            out_specs=[
                pl.BlockSpec(placed.shape, lambda i: (0, 0, 0, 0)),
                pl.BlockSpec((steps, requests, width), lambda i: (0, 0, 0)),
            ],
            out_shape=(placed, jax.ShapeDtypeStruct((steps, requests, width), F32)),
            compiler_params=limited,
        )(handed, decode_hidden)
        return pool, (hidden + delta).astype(BF16)[None]

    def idle_finish(attended, span_kv, handed):
        span = pl.pallas_call(
            copy_kernel, in_specs=[whole], out_specs=whole, out_shape=placed, compiler_params=limited
        )(span_kv)
        return span, jnp.zeros((1, steps, requests, width), BF16)

    return lax.cond(prefill_side, idle_finish, finish, attended, span_kv, handed)


def solution(mesh):
    shape = mesh.devices.shape
    fine = Mesh(mesh.devices.reshape(shape[0], Z, Y, shape[2]), ("role", "z", "y", "tp"))
    placed = (
        P("role", SEQ, None),
        P(),
        P(None, None, "tp"),
        P(),
        P(),
        P(SEQ, "tp"),
        P("tp", SEQ),
        P(None, SEQ, None),
        P(SEQ, None, None, "tp"),
        P(SEQ),
        P(),
        P(),
    )
    return jax.shard_map(
        shards,
        mesh=fine,
        in_specs=placed,
        out_specs=(P("role", SEQ, None, "tp"), P("role", None, SEQ, None)),
        check_vma=False,
    )
```

```python
import math

import jax
import jax.numpy as jnp
from jax import lax
from jax.experimental import pallas as pl
from jax.experimental.pallas import tpu as pltpu
from jax.sharding import Mesh, PartitionSpec as P

QUERY_HEADS = 64
KEY_VALUE_HEADS = 8
HEAD_SIZE = 128
EPSILON = 1e-06
THETA_BASE = 1000000.0

Z, Y = 8, 4
SEQ = ("z", "y")
BLOCK_TOKENS = 8
CAPACITY = 2
VMEM_LIMIT = 8 * 2**20
F32, BF16 = jnp.float32, jnp.bfloat16


def row_scaling(values, weights):
    return values * lax.rsqrt(jnp.mean(values * values, axis=-1, keepdims=True) + EPSILON) * weights


def rotary_tables(token_position):
    half_dim = HEAD_SIZE // 2
    frequency = jnp.exp(
        jnp.arange(half_dim, dtype=F32) * (-2.0 * math.log(THETA_BASE) / HEAD_SIZE)
    )
    angles = token_position.astype(F32)[:, None] * frequency
    return jnp.cos(angles), jnp.sin(angles)


def apply_rotary(values, cosine, sine):
    half_dim = HEAD_SIZE // 2
    first_half = values[..., :half_dim]
    second_half = values[..., half_dim:]
    return jnp.concatenate(
        [first_half * cosine - second_half * sine, second_half * cosine + first_half * sine],
        axis=-1,
    )


def head_norm_rotary(values, gain, cosine, sine):
    rows, width = values.shape
    heads = values.reshape(rows, width // HEAD_SIZE, HEAD_SIZE)
    turned = apply_rotary(row_scaling(heads, gain), cosine[:, None, :], sine[:, None, :])
    return turned.reshape(rows, width)


def dot(a, b):
    return jnp.dot(a, b, preferred_element_type=F32)


def norm_kernel(y_ref, hidden_ref, gain_ref, spread_ref, normed_ref, *unused):
    hidden = jnp.concatenate(
        [hidden_ref[step].astype(F32) for step in range(hidden_ref.shape[0])], axis=0
    )
    normed = row_scaling(hidden, gain_ref[...])
    normed_ref[...] = normed.astype(BF16)
    chunk = spread_ref.shape[2]
    shift = lax.rem(Y - y_ref[0], Y) * (chunk // Y)
    for z in range(Z):
        block = normed[:, z * chunk : (z + 1) * chunk]
        spread_ref[z] = pltpu.roll(block, shift, axis=1).astype(BF16)


TILE = 512


def query_kernel(rows_ref, own_ref, first_ref, second_ref, total_ref):
    depth = 3 * own_ref.shape[0]
    for start in range(0, total_ref.shape[1], TILE):
        columns = slice(start, start + TILE)
        weight = jnp.concatenate(
            [ref[:, columns] for ref in (own_ref, first_ref, second_ref)], axis=0
        )
        total_ref[:, columns] = dot(rows_ref[:, :depth], weight)


def last_query_kernel(rows_ref, total_ref, third_ref, out_ref, last_ref, semaphores):
    depth = 3 * last_ref.shape[0]
    copies = []
    for i in range(out_ref.shape[1] // TILE):
        columns = slice(i * TILE, (i + 1) * TILE)
        copies.append(
            pltpu.make_async_copy(
                third_ref.at[:, columns], last_ref.at[:, columns], semaphores.at[i]
            )
        )
        copies[i].start()
    for i, copy in enumerate(copies):
        columns = slice(i * TILE, (i + 1) * TILE)
        copy.wait()
        last = dot(rows_ref[:, depth:], last_ref[:, columns])
        out_ref[:, columns] = (total_ref[:, columns] + last).astype(BF16)


def attention_kernel(
    length_ref,
    returned_ref,
    gain_ref,
    cosine_ref,
    sine_ref,
    keys_ref,
    values_ref,
    new_keys_ref,
    new_values_ref,
    out_ref,
    *unused,
):
    rows = returned_ref.shape[1]
    requests = rows // 4
    slots, local_width = keys_ref.shape
    context = slots // requests
    group = returned_ref.shape[2] // local_width
    scale = HEAD_SIZE ** (-0.5)
    cosine = jnp.concatenate([cosine_ref[...]] * group, axis=0)
    sine = jnp.concatenate([sine_ref[...]] * group, axis=0)

    def indices(columns):
        row = lax.broadcasted_iota(jnp.int32, (group * rows, columns), 0) % rows
        return row, lax.broadcasted_iota(jnp.int32, (group * rows, columns), 1)

    row, slot = indices(slots)
    request = slot // context
    limit = jnp.full_like(slot, length_ref[0])
    for one in range(1, requests):
        limit = jnp.where(request == one, length_ref[one], limit)
    seen = jnp.logical_and(row % requests == request, slot % context < limit)
    row, new = indices(rows)
    seen_new = jnp.logical_and(
        row % requests == new % requests, new // requests <= row // requests
    )
    for head in range(local_width // HEAD_SIZE):
        columns = slice(head * HEAD_SIZE, (head + 1) * HEAD_SIZE)
        query = []
        for one in range(head * group, (head + 1) * group):
            part = slice(one * HEAD_SIZE, (one + 1) * HEAD_SIZE)
            total = returned_ref[0, :, part].astype(F32)
            for z in range(1, Z):
                total += returned_ref[z, :, part].astype(F32)
            query.append(total)
        query = row_scaling(jnp.concatenate(query, axis=0), gain_ref[...])
        query = query * cosine + pltpu.roll(query, HEAD_SIZE // 2, axis=1) * sine
        query = query.astype(BF16)
        transposed = (((1,), (1,)), ((), ()))
        old = lax.dot_general(
            query, keys_ref[:, columns], transposed, preferred_element_type=F32
        ) * scale
        new = lax.dot_general(
            query, new_keys_ref[:, columns], transposed, preferred_element_type=F32
        ) * scale
        old = jnp.where(seen, old, -jnp.inf)
        new = jnp.where(seen_new, new, -jnp.inf)
        top = jnp.maximum(
            jnp.max(old, axis=-1, keepdims=True), jnp.max(new, axis=-1, keepdims=True)
        )
        old_exp = jnp.exp(old - top)
        new_exp = jnp.exp(new - top)
        total = jnp.sum(old_exp, axis=-1, keepdims=True) + jnp.sum(new_exp, axis=-1, keepdims=True)
        mixed = dot((old_exp / total).astype(BF16), values_ref[:, columns])
        mixed += dot((new_exp / total).astype(BF16), new_values_ref[:, columns])
        mixed = mixed.astype(BF16)
        for one in range(group):
            part = head * group + one
            block = mixed[one * rows : (one + 1) * rows]
            for z in range(Z):
                out_ref[z, :, part * HEAD_SIZE : (part + 1) * HEAD_SIZE] = block


def copy_kernel(source_ref, out_ref):
    out_ref[0] = source_ref[...]


def packed(pool, width):
    sides = width // pool.shape[1]
    run = pool.shape[0] // sides
    return jnp.concatenate([pool[i * run : (i + 1) * run] for i in range(sides)], axis=1)


def unpack_kernel(handed_ref, hidden_ref, out_ref, wide_ref):
    wide_ref[...] = hidden_ref[...].astype(F32)
    tokens, sections, width = out_ref.shape[1:]
    sides = handed_ref.shape[1] // (sections * width)
    run = tokens // sides
    for i in range(sides):
        parts = []
        for section in range(sections):
            start = (i * sections + section) * width
            parts.append(handed_ref[:, start : start + width].astype(F32)[:, None, :])
        run_kv = jnp.concatenate(parts, axis=1).astype(out_ref.dtype)
        out_ref[0, i * run : (i + 1) * run] = run_kv


def shards(
    span_hidden,
    attn_gain,
    kv_weight,
    q_gain,
    key_norm_gain,
    q_weight,
    o_weight,
    decode_hidden,
    cache,
    cache_len,
    block_owner,
    block_slot,
):
    y_index = lax.axis_index("y")
    seq_index = lax.axis_index("z") * Y + y_index
    prefill_side = lax.axis_index("role") == 0
    span_rows = span_hidden.shape[1]
    local_width = kv_weight.shape[2]
    steps, requests, width = decode_hidden.shape
    rows = steps * requests
    depth, local_query = q_weight.shape
    out_depth, out_width = o_weight.shape
    seq_count, block_count = block_owner.shape
    buffer_tokens = seq_count * CAPACITY * BLOCK_TOKENS
    chunk = width // Z
    context = cache.shape[1]
    slots = requests * context
    exchanged = (Z, rows, local_query)

    whole = pl.BlockSpec(memory_space=pltpu.VMEM)
    unwritten = anywhere = pl.BlockSpec(memory_space=pl.ANY)
    section = jax.ShapeDtypeStruct((span_rows, 2, local_width), BF16)
    buffer = jax.ShapeDtypeStruct((seq_count, CAPACITY * BLOCK_TOKENS, 2 * local_width), BF16)

    def rank_table():
        block_number = jnp.arange(block_count, dtype=jnp.int32)
        same_owner = block_owner[:, :, None] == block_owner[:, None, :]
        earlier = block_number[None, None, :] < block_number[None, :, None]
        return jnp.sum(jnp.logical_and(same_owner, earlier).astype(jnp.int32), axis=2)

    pool_rows = span_rows * 2 * local_width // out_depth
    handed_over = jax.ShapeDtypeStruct((Y * out_width + pool_rows, out_depth), BF16)

    def one_hot(blocks):
        token = lax.broadcasted_iota(jnp.int32, (block_count, BLOCK_TOKENS), 1)
        at = (blocks[:, None] * BLOCK_TOKENS + token).reshape(1, span_rows)
        place = lax.broadcasted_iota(jnp.int32, (buffer_tokens, span_rows), 0)
        return (place == at).astype(BF16)

    def prefill(*_):
        normed = row_scaling(span_hidden[0].astype(F32), attn_gain).astype(BF16)
        projected = jnp.einsum("td,dcw->ctw", normed, kv_weight, preferred_element_type=F32)
        cosine, sine = rotary_tables(seq_index * span_rows + jnp.arange(span_rows, dtype=jnp.int32))
        keys = head_norm_rotary(projected[0], key_norm_gain, cosine, sine)
        span_kv = jnp.concatenate([keys, projected[1]], axis=1).astype(BF16)
        own_owner = lax.dynamic_index_in_dim(block_owner, seq_index, 0, keepdims=False)
        own_rank = lax.dynamic_index_in_dim(rank_table(), seq_index, 0, keepdims=False)
        payload = dot(one_hot(own_owner * CAPACITY + own_rank), span_kv).astype(BF16)
        return (
            jnp.zeros((Z * rows, chunk), BF16),
            jnp.zeros((rows, HEAD_SIZE), F32),
            jnp.zeros((rows, HEAD_SIZE), F32),
            jnp.zeros((rows, local_width), BF16),
            jnp.zeros((rows, local_width), BF16),
            jnp.zeros((slots, local_width), BF16),
            jnp.zeros((slots, local_width), BF16),
            span_kv.reshape(section.shape),
            payload.reshape(buffer.shape),
        )

    def route(payload, *_):
        turned = o_weight.T
        handed = jnp.zeros(handed_over.shape, BF16)
        for shift in range(Y):
            part = turned
            if shift > 0:
                part = lax.ppermute(turned, "y", [(i, (i - shift) % Y) for i in range(Y)])
            handed = lax.dynamic_update_slice(
                handed, part, (lax.rem(y_index + shift, Y) * out_width, 0)
            )
        arrived = lax.all_to_all(payload, SEQ, split_axis=0, concat_axis=0, tiled=True)
        block_number = jnp.arange(block_count, dtype=jnp.int32)
        came_as = jnp.arange(seq_count, dtype=jnp.int32)[:, None] * CAPACITY + rank_table()
        target = jnp.where(block_owner == seq_index, block_slot, -1)
        source = jnp.sum(
            jnp.where(target[None] == block_number[:, None, None], came_as[None], 0), axis=(1, 2)
        )
        pool = lax.dot_general(
            one_hot(source),
            arrived.reshape(buffer_tokens, 2 * local_width),
            (((0,), (0,)), ((), ())),
            preferred_element_type=F32,
        ).astype(BF16)
        handed = lax.dynamic_update_slice(handed, packed(pool, out_depth), (Y * out_width, 0))
        return handed, jnp.zeros(exchanged, BF16)

    arrived_weights = [None] * (Y - 1)
    for shift in (2, 3, 1):
        pairs = [(i, Y + (i - shift) % Y) for i in range(Y)] + [(Y + i, i) for i in range(Y)]
        arrived_weights[shift - 1] = lax.ppermute(q_weight, ("role", "y"), pairs)

    def project(*_):
        spread, normed, span_kv, payload = pl.pallas_call(
            norm_kernel,
            out_shape=(
                jax.ShapeDtypeStruct((Z, rows, chunk), BF16),
                jax.ShapeDtypeStruct((rows, width), BF16),
                section,
                buffer,
            ),
            in_specs=[
                pl.BlockSpec(memory_space=pltpu.SMEM),
                whole,
                whole,
            ],
            out_specs=[whole] * 2 + [unwritten] * 2,
            compiler_params=pltpu.CompilerParams(vmem_limit_bytes=VMEM_LIMIT),
        )(y_index.astype(jnp.int32).reshape(1), decode_hidden, attn_gain.reshape(1, width))
        spread = lax.all_to_all(spread, "z", split_axis=0, concat_axis=0, tiled=True)
        position = (
            cache_len[None, :] + jnp.arange(steps, dtype=jnp.int32)[:, None]
        ).reshape(rows)
        cosine, sine = rotary_tables(position)
        fresh = jnp.einsum("rd,dcw->crw", normed, kv_weight, preferred_element_type=F32)
        new_keys = head_norm_rotary(fresh[0], key_norm_gain, cosine, sine).astype(BF16)
        new_values = fresh[1].astype(BF16)
        cosine = jnp.concatenate([cosine, cosine], axis=1)
        sine = jnp.concatenate([-sine, sine], axis=1)
        spread = spread.reshape(Z * rows, chunk)
        keys = cache[:, :, 0].reshape(slots, local_width)
        values = cache[:, :, 1].reshape(slots, local_width)
        return spread, cosine, sine, new_keys, new_values, keys, values, span_kv, payload

    spread, *beside, span_kv, payload = lax.cond(prefill_side, prefill, project)

    total = pl.pallas_call(
        query_kernel,
        in_specs=[whole] * 4,
        out_specs=whole,
        out_shape=jax.ShapeDtypeStruct((Z * rows, local_query), F32),
        compiler_params=pltpu.CompilerParams(vmem_limit_bytes=VMEM_LIMIT),
    )(spread, q_weight, *arrived_weights[:2])

    def attend(payload, spread, cosine, sine, new_keys, new_values, keys, values, total, last):
        partial = pl.pallas_call(
            last_query_kernel,
            in_specs=[whole] * 2 + [anywhere],
            out_specs=whole,
            out_shape=jax.ShapeDtypeStruct((Z * rows, local_query), BF16),
            scratch_shapes=[
                pltpu.VMEM((depth, local_query), BF16),
                pltpu.SemaphoreType.DMA((local_query // TILE,)),
            ],
            compiler_params=pltpu.CompilerParams(vmem_limit_bytes=VMEM_LIMIT),
        )(spread, total, last)
        returned = lax.all_to_all(
            partial.reshape(exchanged), "z", split_axis=0, concat_axis=0, tiled=True
        )
        attended, handed = pl.pallas_call(
            attention_kernel,
            out_shape=(
                jax.ShapeDtypeStruct(exchanged, BF16),
                handed_over,
            ),
            in_specs=[pl.BlockSpec(memory_space=pltpu.SMEM)] + [whole] * 8,
            out_specs=[whole, unwritten],
            compiler_params=pltpu.CompilerParams(vmem_limit_bytes=VMEM_LIMIT),
        )(
            cache_len,
            returned,
            q_gain.reshape(1, HEAD_SIZE),
            cosine,
            sine,
            keys,
            values,
            new_keys,
            new_values,
        )
        return handed, attended

    handed, attended = lax.cond(
        prefill_side, route, attend,
        payload, spread, *beside, total, arrived_weights[2],
    )
    handed = lax.ppermute(handed, "role", [(0, 1)])

    def gather(attended):
        return lax.all_to_all(attended, "z", split_axis=0, concat_axis=0, tiled=True)

    attended = lax.cond(prefill_side, lambda attended: attended, gather, attended)

    limited = pltpu.CompilerParams(vmem_limit_bytes=VMEM_LIMIT)
    placed = jax.ShapeDtypeStruct((1,) + section.shape, BF16)

    def finish(attended, span_kv, handed):
        partial = lax.dot_general(
            attended.reshape(Z * rows, local_query),
            handed,
            (((1,), (1,)), ((), ())),
            preferred_element_type=F32,
        )[:, : Y * out_width].astype(BF16)
        back = lax.all_to_all(
            partial.reshape(Z, rows, chunk), "z", split_axis=0, concat_axis=0, tiled=True
        )
        tp_count = lax.axis_size("tp")
        delta = back.astype(F32)
        for shift in sorted(range(1, tp_count), key=lambda shift: -min(shift, tp_count - shift)):
            pairs = [(i, (i + shift) % tp_count) for i in range(tp_count)]
            delta = delta + lax.ppermute(back, "tp", pairs).astype(F32)
        delta = delta.transpose(1, 0, 2).reshape(steps, requests, width)
        pool, hidden = pl.pallas_call(
            unpack_kernel,
            grid=(1,),
            in_specs=[
                pl.BlockSpec((pool_rows, out_depth), lambda i: (Y * out_width // pool_rows, 0)),
                pl.BlockSpec((steps, requests, width), lambda i: (0, 0, 0)),
            ],
            out_specs=[
                pl.BlockSpec(placed.shape, lambda i: (0, 0, 0, 0)),
                pl.BlockSpec((steps, requests, width), lambda i: (0, 0, 0)),
            ],
            out_shape=(placed, jax.ShapeDtypeStruct((steps, requests, width), F32)),
            compiler_params=limited,
        )(handed, decode_hidden)
        return pool, (hidden + delta).astype(BF16)[None]

    def idle_finish(attended, span_kv, handed):
        span = pl.pallas_call(
            copy_kernel, in_specs=[whole], out_specs=whole, out_shape=placed, compiler_params=limited
        )(span_kv)
        return span, jnp.zeros((1, steps, requests, width), BF16)

    return lax.cond(prefill_side, idle_finish, finish, attended, span_kv, handed)


def solution(mesh):
    shape = mesh.devices.shape
    fine = Mesh(mesh.devices.reshape(shape[0], Z, Y, shape[2]), ("role", "z", "y", "tp"))
    placed = (
        P("role", SEQ, None),
        P(),
        P(None, None, "tp"),
        P(),
        P(),
        P(SEQ, "tp"),
        P("tp", SEQ),
        P(None, SEQ, None),
        P(SEQ, None, None, "tp"),
        P(SEQ),
        P(),
        P(),
    )
    return jax.shard_map(
        shards,
        mesh=fine,
        in_specs=placed,
        out_specs=(P("role", SEQ, None, "tp"), P("role", None, SEQ, None)),
        check_vma=False,
    )
```
